256 devices in a mesh: dp: 8 (over y, core), expert: 8 (over x, z_hi), mp: 4 (over z_lo).
Axes of the slice: x: 4, y: 4, z: 8 (z_hi: 2, z_lo: 4; z = z_hi * 4 + z_lo), core: 2. Of those that a mesh axis runs over, the one named last changes fastest.
Arguments:
- tokens: bfloat16 [1024, 4096], P('dp', ('expert', 'mp')), may hold values from -6 to 6
- cotangent: bfloat16 [1024, 4096], P('dp', ('expert', 'mp')), may hold values from -6 to 6
- gates: float32 [1024, 2], P('dp'), may hold values from 0.2 to 1
- expert_ids: int32 [1024, 2], P('dp'), may hold values from 0 to 7, all different within a row; in each aligned block of 128 rows (0 to 127, 128 to 255, ...) at most 48 rows name the same one
- dense_ffn: bfloat16 [3, 4096, 8192], P(None, 'expert', ('dp', 'mp')), may hold values from -0.09375 to 0.09375
- redrawn: int32 [8, 8192], P(None, ('dp', 'mp')), may hold values from 0 to 1, as said below
- redraw: bfloat16 [8, 3, 4096, 4096], P('expert', None, None, ('dp', 'mp')), may hold values from -0.09375 to 0.09375
Outputs:
- mixed: bfloat16 [1024, 4096], P('dp', ('expert', 'mp'))
- token_grad: bfloat16 [1024, 4096], P('dp', ('expert', 'mp'))
- new_weights: bfloat16 [8, 3, 4096, 8192], P('expert', None, None, ('dp', 'mp'))
The draws below stay inside these ranges and needn't reach their ends.
Inputs may be any that keep to these rules, and one draw needn't show every extreme that they name: `expert_ids`: the two experts of a token differ; in every aligned block of 128 tokens each expert is named by at most 48 tokens, and in some block one expert by exactly 48. `redrawn`: in every expert, exactly half of every aligned block of 256 hidden units is 1.
All inputs are finite; a program needn't handle non-finite values.
Results may differ from the reference program's by a relative error of at most 0.023.
Values may be sent and summed in bfloat16 or wider, within the bound.
No kernel may reach another device: no remote copies, remote signals or barrier semaphores. Data moves between devices by JAX's collectives and lax.ppermute only.
A program may use at most 128 MiB of HBM per device.

```python
import math
import jax
import jax.numpy as jnp
import numpy as np
from jax import lax

D = 4096
FF = 8192
TOP = 2
TOK_DEV = 128
E = 8
TOKENS = 1024
CAP = 48
EXPERT_ROWS = 384
COLS_DEV = 256
N_DP = 8


def draw_redrawn(key, part):
    key = jax.random.fold_in(key, 11)
    blocks = E * (FF // COLS_DEV)
    noise = jax.random.randint(key, (blocks, COLS_DEV), 0, 2 ** 20, dtype=jnp.int32)
    scores = noise * COLS_DEV + jnp.arange(COLS_DEV, dtype=jnp.int32)[None, :]
    places = jnp.argsort(jnp.argsort(scores, axis=1), axis=1)
    marks = (places < COLS_DEV // 2).astype(jnp.int32)
    return marks.reshape(E, FF)


def level_of(stream_key, shape, pieces, least, largest):
    def one(position, blocks):
        heights = jax.random.uniform(jax.random.fold_in(jax.random.fold_in(stream_key, 6), position), (blocks,), jnp.float32, least / len(pieces), largest / len(pieces))
        return jnp.repeat(jnp.exp(heights), shape[position] // blocks).reshape((-1,) + (1,) * (len(shape) - position - 1))

    level = one(*pieces[0])
    for cut in pieces[1:]:
        level = level * one(*cut)
    return level


def assign_block(rng, own, number, rows, count, top, limit, slope):
    order = jax.random.permutation(rng, count)
    packed, common = load_shares(count, rows * top, limit, slope, True), load_shares(count, rows * top, limit, slope, False)
    places = jnp.arange(count)

    def named(lengths, offset_by):
        used = int((lengths > 0).sum())
        fixed = max(1, used // 4)
        moved = fixed + (places - fixed + offset_by * (used - fixed)) % max(1, count - fixed)
        return jnp.zeros((count,), jnp.int32).at[order[jnp.where(places < fixed, places, moved)]].set(jnp.asarray(lengths, jnp.int32))

    lengths = jnp.where(number % 4 == 0, named(packed, number // 4), named(common, number - number // 4 - 1))
    mixed = jax.random.permutation(jax.random.fold_in(own, 3), count)
    donor, sink = mixed[0:count // 2 * 2:2], mixed[1:count // 2 * 2:2]
    slack = jnp.minimum(lengths[donor] - 1, limit - lengths[sink]) // 2
    slack = jnp.where((donor == order[0]) | (sink == order[0]) | (lengths[sink] == 0), 0, jnp.maximum(slack, 0))
    moved = jax.random.randint(jax.random.fold_in(own, 4), (count // 2,), 0, 1 << 20) % (slack + 1)
    lengths = lengths.at[donor].add(-moved).at[sink].add(moved)
    items = jnp.searchsorted(jnp.cumsum(lengths), jnp.arange(rows * top), side="right").astype(jnp.int32)
    table = items.reshape(top, rows).T
    table = table[jax.random.permutation(jax.random.fold_in(own, 1), rows)]
    offset_by = jax.random.randint(jax.random.fold_in(own, 2), (rows, 1), 0, top)
    return jnp.take_along_axis(table, (jnp.arange(top)[None, :] + offset_by) % top, axis=1)


def load_shares(number_of, total, limit, slope, full):
    portions = [(1 << 20) // math.isqrt(grade ** slope) + 1 for grade in range(1, number_of + 1)]
    largest = limit if full else min(limit, max(-(-total // number_of), total * portions[0] // sum(portions)))
    least = 1 if total - largest >= number_of - 1 else 0
    given, spare = [largest] + [least] * (number_of - 1), total - largest - least * (number_of - 1)
    while spare > 0:
        free = [i for i in range(1, number_of) if given[i] < largest] or [i for i in range(1, number_of) if given[i] < limit]
        whole, left = sum([portions[i] for i in free]), spare
        for i in free:
            more = min(limit - given[i], max(1, left * portions[i] // whole), spare)
            given[i] = given[i] + more
            spare = spare - more
    return np.array(given)


def normal_values(stream_key, extent, width, bound, split=(), kind=jnp.bfloat16):
    values = width * jax.random.normal(stream_key, extent, jnp.float32)
    if split:
        values = values * level_of(stream_key, extent, split, -0.22, 0.18)
    return jnp.clip(values, -bound, bound).astype(kind)


def setup_inputs(seed: int = 0) -> dict:
    seeds = jax.random.split(jax.random.key(seed), 8)
    tokens = normal_values(seeds[0], (TOKENS, D), 1.0, 6.0, ((0, 8), (1, 32)))
    cotangent = normal_values(seeds[1], (TOKENS, D), 1.0, 6.0, ((0, 8), (1, 32)))
    gates = jnp.clip(0.2 + 0.8 * jax.random.uniform(seeds[2], (TOKENS, TOP), jnp.float32) ** level_of(seeds[2], (TOKENS, TOP), ((0, 8),), -0.2, 0.2), 0.2, 1.0)
    expert_ids_keys = jax.random.split(jax.random.fold_in(seeds[3], 1), TOKENS // TOK_DEV)
    expert_ids_turns = jax.random.permutation(jax.random.fold_in(seeds[3], 3), TOKENS // TOK_DEV)
    expert_ids = jax.vmap(lambda own, number: assign_block(jax.random.fold_in(seeds[3], 2), own, number, TOK_DEV, E, TOP, CAP, 2))(expert_ids_keys, expert_ids_turns).reshape((TOKENS, TOP))
    dense_ffn = normal_values(seeds[4], (3, D, FF), D ** -0.5, 0.09375, ((1, 8), (2, 32)))
    redrawn = draw_redrawn(jax.random.fold_in(seeds[7], 71), 0)
    redraw = normal_values(seeds[6], (E, 3, D, FF // 2), D ** -0.5, 0.09375, ((0, 8), (3, 32)))
    return {"tokens": tokens, "cotangent": cotangent, "gates": gates, "expert_ids": expert_ids, "dense_ffn": dense_ffn, "redrawn": redrawn, "redraw": redraw}


def assign_rows(expert_ids):
    flat_ids = expert_ids.reshape(N_DP, TOK_DEV * TOP).astype(jnp.int32)
    onehot = (flat_ids[:, :, None] == jnp.arange(E, dtype=jnp.int32)[None, None, :]).astype(jnp.int32)
    before = jnp.cumsum(onehot, axis=1).astype(jnp.int32) - onehot
    slot_num = jnp.sum(before * onehot, axis=2).astype(jnp.int32)
    block_num = jnp.arange(N_DP, dtype=jnp.int32)[:, None]
    target = flat_ids * EXPERT_ROWS + block_num * CAP + slot_num
    return target.reshape(-1).astype(jnp.int32)


def blocked_sum(lefts, rights):
    groups = FF // COLS_DEV
    rows = lefts[0].shape[0]

    def step(total, group):
        start = (group * COLS_DEV).astype(jnp.int32)
        term = jnp.zeros((rows, D), jnp.float32)
        for left, right in zip(lefts, rights):
            piece_left = lax.dynamic_slice_in_dim(left, start, COLS_DEV, 1)
            piece_right = lax.dynamic_slice_in_dim(right, start, COLS_DEV, 1)
            term = term + jnp.dot(piece_left, piece_right.T, preferred_element_type=jnp.float32)
        rounded = lax.optimization_barrier(term.astype(jnp.bfloat16))
        return total + rounded.astype(jnp.float32), None

    total, unused = lax.scan(step, jnp.zeros((rows, D), jnp.float32), jnp.arange(groups, dtype=jnp.int32))
    return total


def expert_pass(weights, expert_in, expert_cot):
    w_gate, w_up, w_down = weights[0], weights[1], weights[2]
    gate_act = jnp.dot(expert_in, w_gate, preferred_element_type=jnp.float32)
    up_act = jnp.dot(expert_in, w_up, preferred_element_type=jnp.float32)
    sig = jax.nn.sigmoid(gate_act)
    act = gate_act * sig
    hidden = (act * up_act).astype(jnp.bfloat16)
    expert_out = blocked_sum([hidden], [w_down])
    hidden_grad = jnp.dot(expert_cot, w_down, preferred_element_type=jnp.float32)
    gate_grad = (hidden_grad * up_act * sig * (1.0 + gate_act * (1.0 - sig))).astype(jnp.bfloat16)
    up_grad = (hidden_grad * act).astype(jnp.bfloat16)
    in_grad = blocked_sum([gate_grad, up_grad], [w_gate, w_up])
    grad_gate = jnp.dot(expert_in.T, gate_grad, preferred_element_type=jnp.float32)
    grad_up = jnp.dot(expert_in.T, up_grad, preferred_element_type=jnp.float32)
    grad_down = jnp.dot(expert_cot.T, hidden, preferred_element_type=jnp.float32)
    return expert_out, in_grad, jnp.stack([grad_gate, grad_up, grad_down])


def adamw_step(weights, grads):
    update = grads / (jnp.abs(grads) + 0.1)
    return (weights.astype(jnp.float32) * (1.0 - 0.0003) - 0.003 * update).astype(jnp.bfloat16)


def reference(tokens, cotangent, gates, expert_ids, dense_ffn, redrawn, redraw):
    target = assign_rows(expert_ids)
    total_rows = E * EXPERT_ROWS
    token_rep = jnp.repeat(tokens, TOP, axis=0)
    cot_rep = (gates.reshape(-1, 1) * jnp.repeat(cotangent, TOP, axis=0).astype(jnp.float32)).astype(jnp.bfloat16)
    expert_in = jnp.zeros((total_rows, D), jnp.bfloat16).at[target].set(token_rep).reshape(E, EXPERT_ROWS, D)
    expert_cot = jnp.zeros((total_rows, D), jnp.bfloat16).at[target].set(cot_rep).reshape(E, EXPERT_ROWS, D)
    ranks = jnp.clip(jnp.cumsum(redrawn, axis=1).astype(jnp.int32) - 1, 0, FF // 2 - 1).astype(jnp.int32)

    def one_expert(items):
        mask_row, rank_row, fresh, rows_in, rows_cot = items
        taken = jnp.take(fresh, rank_row, axis=2)
        weights = jnp.where(mask_row[None, None, :] == 1, taken, dense_ffn)
        expert_out, in_grad, grads = expert_pass(weights, rows_in, rows_cot)
        return expert_out, in_grad, adamw_step(weights, grads)

    outs, in_grads, new_weights = lax.map(one_expert, (redrawn, ranks, redraw, expert_in, expert_cot))
    out_rows = outs.reshape(total_rows, D)[target].reshape(TOKENS, TOP, D)
    grad_rows = in_grads.reshape(total_rows, D)[target].reshape(TOKENS, TOP, D)
    mixed = jnp.sum(gates[:, :, None] * out_rows, axis=1).astype(jnp.bfloat16)
    token_grad = jnp.sum(grad_rows, axis=1).astype(jnp.bfloat16)
    return mixed, token_grad, new_weights
```

```python
import jax
import jax.numpy as jnp
from jax import lax
from jax.experimental import pallas as pl
from jax.experimental.pallas import tpu as pltpu
from jax.sharding import PartitionSpec as P

BF = jnp.bfloat16
F32 = jnp.float32
CAP = 48
N_E = 8
N_DP = 8
N_MP = 4
N_X = 4
LANE = 128
COLS = 256
HALF = 128
SLAB = 512
TOK = 128
ROWS = N_DP * CAP
VMEM_CAP = 56 * 1024 * 1024


def iota(shape, dim):
    return lax.broadcasted_iota(jnp.int32, shape, dim)


def dot_nn(a, b):
    return lax.dot_general(a, b, (((1,), (0,)), ((), ())), preferred_element_type=F32)


def dot_nt(a, b):
    return lax.dot_general(a, b, (((1,), (1,)), ((), ())), preferred_element_type=F32)


def dot_tn(a, b):
    return lax.dot_general(a, b, (((0,), (0,)), ((), ())), preferred_element_type=F32)


def tables(ids_ref):
    lane = iota((TOK, LANE), 1)
    hits = [(ids_ref[:, j : j + 1] == lane).astype(F32) for j in range(2)]
    earlier = (iota((TOK, TOK), 1) < iota((TOK, TOK), 0)).astype(BF)
    rank = dot_nn(earlier, (hits[0] + hits[1]).astype(BF))
    slot = iota((TOK, N_E * CAP), 1)
    out = []
    for j in range(2):
        place = jnp.sum(hits[j] * (rank + (lane * CAP).astype(F32)), axis=1, keepdims=True)
        out.append((slot == place.astype(jnp.int32)).astype(F32))
    return out


def dispatch_kernel(ids_ref, gates_ref, tok_ref, cot_ref, out_ref):
    t0, t1 = tables(ids_ref)
    rows_in = dot_tn((t0 + t1).astype(BF), tok_ref[...]).astype(BF)
    cot = cot_ref[...].astype(F32)
    scaled0 = (gates_ref[:, 0:1] * cot).astype(BF)
    scaled1 = (gates_ref[:, 1:2] * cot).astype(BF)
    rows_cot = (dot_tn(t0.astype(BF), scaled0) + dot_tn(t1.astype(BF), scaled1)).astype(BF)
    for e in range(N_E):
        out_ref[e, 0:CAP, :] = rows_in[e * CAP : (e + 1) * CAP]
        out_ref[e, CAP : 2 * CAP, :] = rows_cot[e * CAP : (e + 1) * CAP]


def combine_kernel(ids_ref, gates_ref, back_ref, mixed_ref, grad_ref):
    t0, t1 = tables(ids_ref)
    total = back_ref[:, 0].astype(F32)
    for q in range(1, N_MP):
        total = total + back_ref[:, q].astype(F32)
    out = total[:, 0:CAP].reshape(N_E * CAP, LANE)
    grad = total[:, CAP : 2 * CAP].reshape(N_E * CAP, LANE)
    high = lax.Precision.HIGHEST
    weighted = t0 * gates_ref[:, 0:1] + t1 * gates_ref[:, 1:2]
    mixed_ref[...] = jnp.dot(weighted, out, precision=high, preferred_element_type=F32).astype(BF)
    grad_ref[...] = jnp.dot(t0 + t1, grad, precision=high, preferred_element_type=F32).astype(BF)


def counts(marks_ref):
    upto = (iota((COLS, COLS), 0) <= iota((COLS, COLS), 1)).astype(BF)
    return dot_nn(marks_ref[...].astype(BF), upto)


def pick_row(values, row):
    return jnp.sum(jnp.where(iota(values.shape, 0) == row, values, 0.0), axis=0, keepdims=True)


def pack_kernel(where_ref, marks_ref, dense_ref, *outs):
    cum = counts(marks_ref)
    marks = marks_ref[...].astype(F32)
    col = iota((1, COLS), 1).astype(F32)
    dense = dense_ref[...]
    for k in range(N_X):
        expert = lax.rem(where_ref[0] + k, N_X) * 2 + where_ref[1]
        kept = jnp.where(pick_row(marks, expert) > 0.5, -1.0, col - pick_row(cum, expert))
        onehot = (iota((HALF, COLS), 0) == kept.astype(jnp.int32)).astype(BF)
        outs[k][...] = dot_nt(dense, onehot).astype(BF)


def weights_kernel(where_ref, marks_ref, fresh_ref, *refs):
    pieces, out_ref = refs[:-1], refs[-1]
    expert = where_ref[0] * 2 + where_ref[1]
    cum = pick_row(counts(marks_ref), expert)
    mark = pick_row(marks_ref[...].astype(F32), expert)
    col = iota((1, COLS), 1).astype(F32)
    source = jnp.where(mark > 0.5, HALF + cum - 1.0, col - cum).astype(jnp.int32)
    onehot = (iota((COLS, COLS), 0) == source).astype(BF)
    for s, piece in enumerate(pieces):
        side, k = divmod(s, N_X)
        slab = lax.rem(where_ref[0] + N_X - k, N_X) * 2 + (where_ref[1] if side == 0 else 1 - where_ref[1])
        place = pl.ds(pl.multiple_of(slab * SLAB, SLAB), SLAB)
        both = jnp.concatenate([piece[0], fresh_ref[0, place, :]], axis=1)
        out_ref[0, place, :] = dot_nn(both, onehot).astype(BF)


def expert_kernel(rows_ref, w_ref, acts_ref, out_ref, gate_acc, up_acc, down_acc):
    step = pl.program_id(0)

    @pl.when(step < N_MP)
    def _():
        rows = rows_ref[:, 0]
        rin = jnp.concatenate([rows[:, e, 0:CAP].reshape(ROWS, LANE) for e in range(N_E)], axis=1)
        rcot = jnp.concatenate(
            [rows[:, e, CAP : 2 * CAP].reshape(ROWS, LANE) for e in range(N_E)], axis=1
        )
        parts = (
            dot_nn(rin, w_ref[0, :, 0].reshape(N_E * LANE, COLS)),
            dot_nn(rin, w_ref[1, :, 0].reshape(N_E * LANE, COLS)),
            dot_nn(rcot, w_ref[2, :, 0].reshape(N_E * LANE, COLS)),
        )

        @pl.when(step == 0)
        def _():
            for acc, part in zip((gate_acc, up_acc, down_acc), parts):
                acc[...] = part

        @pl.when(step > 0)
        def _():
            for acc, part in zip((gate_acc, up_acc, down_acc), parts):
                acc[...] += part

        @pl.when(step == N_MP - 1)
        def _():
            gate, up, grad = gate_acc[...], up_acc[...], down_acc[...]
            sig = jax.nn.sigmoid(gate)
            act = gate * sig
            acts_ref[:, 0:COLS] = (grad * up * sig * (1.0 + gate * (1.0 - sig))).astype(BF)
            acts_ref[:, COLS : 2 * COLS] = (grad * act).astype(BF)
            acts_ref[:, 2 * COLS :] = (act * up).astype(BF)

    @pl.when(step >= N_MP)
    def _():
        pair = jnp.concatenate(
            [w_ref[p, :, 0].reshape(N_E * LANE, COLS) for p in range(2)], axis=1
        )
        out = dot_nt(acts_ref[:, 2 * COLS :], w_ref[2, :, 0].reshape(N_E * LANE, COLS)).astype(BF)
        grad = dot_nt(acts_ref[:, 0 : 2 * COLS], pair).astype(BF)
        for e in range(N_E):
            lanes = slice(e * LANE, (e + 1) * LANE)
            out_ref[:, e, 0, 0:CAP, :] = out[:, lanes].reshape(N_DP, CAP, LANE)
            out_ref[:, e, 0, CAP : 2 * CAP, :] = grad[:, lanes].reshape(N_DP, CAP, LANE)


def update_kernel(rows_ref, acts_ref, w_ref, new_ref):
    for e in range(N_E):
        rin = rows_ref[:, 0, e, 0:CAP].reshape(ROWS, LANE)
        rcot = rows_ref[:, 0, e, CAP : 2 * CAP].reshape(ROWS, LANE)
        pair = dot_tn(rin, acts_ref[:, 0 : 2 * COLS])
        grads = (pair[:, 0:COLS], pair[:, COLS:], dot_tn(rcot, acts_ref[:, 2 * COLS :]))
        for p in range(3):
            g = grads[p]
            new = w_ref[p, e, 0].astype(F32) * (1.0 - 0.0003) - 0.003 * (g / (jnp.abs(g) + 0.1))
            new_ref[p, e, 0] = new.astype(BF)


def call(kernel, outs, flops=0, nbytes=0, **kw):
    return pl.pallas_call(
        kernel,
        out_shape=outs,
        compiler_params=pltpu.CompilerParams(vmem_limit_bytes=VMEM_CAP),
        cost_estimate=pl.CostEstimate(flops=flops, bytes_accessed=nbytes, transcendentals=0),
        **kw,
    )


def sds(shape, dtype=BF):
    return jax.ShapeDtypeStruct(shape, dtype)


SMEM = pl.BlockSpec(memory_space=pltpu.SMEM)


def on_device(tokens, cotangent, gates, expert_ids, dense_ffn, redrawn, redraw):
    expert = lax.axis_index("expert")
    where = jnp.stack([expert // 2, expert % 2]).astype(jnp.int32)

    def along_x(piece, k):
        return lax.ppermute(
            piece, "expert", [(e, (e // 2 + k) % N_X * 2 + e % 2) for e in range(N_E)]
        )

    dense = dense_ffn.reshape(3 * SLAB, COLS)
    pack = call(
        pack_kernel,
        [sds((3 * SLAB, HALF))] * N_X,
        flops=2 * 3 * SLAB * COLS * HALF * N_X,
        nbytes=6 * 3 * SLAB * COLS,
        in_specs=[SMEM, pl.BlockSpec(), pl.BlockSpec()],
    )
    far = lax.ppermute(dense, "expert", [(e, e ^ 1) for e in range(N_E)])
    pieces = []
    for slab in (dense, far):
        packed = pack(where, redrawn, slab)
        pieces += [packed[0]] + [along_x(packed[k], k) for k in range(1, N_X)]
    pieces = [p.reshape(3, SLAB, HALF) for p in pieces]

    slots = call(dispatch_kernel, sds((N_E, 2 * CAP, LANE)), nbytes=400000)(
        expert_ids, gates, tokens, cotangent
    )
    rows = lax.all_to_all(
        slots.reshape(N_E * 2 * CAP, LANE), "expert", split_axis=0, concat_axis=0, tiled=True
    )
    rows = lax.all_gather(rows, "mp", axis=0, tiled=True)
    rows = lax.all_gather(rows, "dp", axis=0, tiled=True)
    rows = rows.reshape(N_DP, N_MP, N_E, 2 * CAP, LANE)

    weights = call(
        weights_kernel,
        sds((3, N_E * SLAB, COLS)),
        flops=2 * 3 * N_E * SLAB * COLS * COLS,
        nbytes=2 * 2 * 3 * N_E * SLAB * COLS,
        grid=(3,),
        in_specs=[
            SMEM,
            pl.BlockSpec((N_E, COLS), lambda p: (0, 0)),
            pl.BlockSpec((1, N_E * SLAB, HALF), lambda p: (p, 0, 0)),
        ]
        + [pl.BlockSpec((1, SLAB, HALF), lambda p: (p, 0, 0))] * (2 * N_X),
        out_specs=pl.BlockSpec((1, N_E * SLAB, COLS), lambda p: (p, 0, 0)),
    )(where, redrawn, redraw[0], *pieces)
    weights = weights.reshape(3, N_E, N_MP, LANE, COLS)

    flops = 2 * ROWS * N_E * SLAB * COLS * 3
    acts, outs = call(
        expert_kernel,
        [sds((ROWS, 3 * COLS)), sds((N_DP, N_E, N_MP, 2 * CAP, LANE))],
        flops=2 * flops,
        nbytes=25000000,
        grid=(2 * N_MP,),
        in_specs=[
            pl.BlockSpec(
                (N_DP, 1, N_E, 2 * CAP, LANE), lambda i: (0, jnp.minimum(i, N_MP - 1), 0, 0, 0)
            ),
            pl.BlockSpec((3, N_E, 1, LANE, COLS), lambda i: (0, 0, lax.rem(i, N_MP), 0, 0)),
        ],
        out_specs=[
            pl.BlockSpec((ROWS, 3 * COLS), lambda i: (0, 0)),
            pl.BlockSpec(
                (N_DP, N_E, 1, 2 * CAP, LANE), lambda i: (0, 0, jnp.maximum(i - N_MP, 0), 0, 0)
            ),
        ],
        scratch_shapes=[pltpu.VMEM((ROWS, COLS), F32)] * 3,
    )(rows, weights)

    part = lax.psum_scatter(
        outs.reshape(N_DP * N_E * N_MP * 2 * CAP, LANE), "dp", scatter_dimension=0, tiled=True
    )
    back = lax.all_to_all(part, ("expert", "mp"), split_axis=0, concat_axis=0, tiled=True)

    new_weights = call(
        update_kernel,
        sds((3, N_E, N_MP, LANE, COLS)),
        flops=flops,
        nbytes=19000000,
        grid=(N_MP,),
        in_specs=[
            pl.BlockSpec((N_DP, 1, N_E, 2 * CAP, LANE), lambda i: (0, i, 0, 0, 0)),
            pl.BlockSpec((ROWS, 3 * COLS), lambda i: (0, 0)),
            pl.BlockSpec((3, N_E, 1, LANE, COLS), lambda i: (0, 0, i, 0, 0)),
        ],
        out_specs=pl.BlockSpec((3, N_E, 1, LANE, COLS), lambda i: (0, 0, i, 0, 0)),
    )(rows, acts, weights)

    mixed, token_grad = call(combine_kernel, [sds((TOK, LANE))] * 2, nbytes=900000)(
        expert_ids, gates, back.reshape(N_E, N_MP, 2 * CAP, LANE)
    )
    return (mixed, token_grad, new_weights.reshape(1, 3, N_E * SLAB, COLS))


def solution(mesh):
    return jax.shard_map(
        on_device,
        mesh=mesh,
        in_specs=(
            P("dp", ("expert", "mp")),
            P("dp", ("expert", "mp")),
            P("dp", None),
            P("dp", None),
            P(None, "expert", ("dp", "mp")),
            P(None, ("dp", "mp")),
            P("expert", None, None, ("dp", "mp")),
        ),
        out_specs=(
            P("dp", ("expert", "mp")),
            P("dp", ("expert", "mp")),
            P("expert", None, None, ("dp", "mp")),
        ),
        check_vma=False,
    )
```

```python
import jax
import jax.numpy as jnp
from jax import lax
from jax.experimental import pallas as pl
from jax.experimental.pallas import tpu as pltpu
from jax.sharding import PartitionSpec as P

BF = jnp.bfloat16
F32 = jnp.float32
CAP = 48
N_E = 8
N_DP = 8
N_X = 4
LANE = 128
COLS = 256
HALF = 128
SLAB = 512
TOK = 128
ROWS = N_DP * CAP
VMEM_CAP = 60 * 1024 * 1024
N_Y = 4
N_Q = 4
PIECE = N_E * N_Q * CAP


def iota(shape, dim):
    return lax.broadcasted_iota(jnp.int32, shape, dim)


def dot_nn(a, b):
    return lax.dot_general(a, b, (((1,), (0,)), ((), ())), preferred_element_type=F32)


def dot_nt(a, b):
    return lax.dot_general(a, b, (((1,), (1,)), ((), ())), preferred_element_type=F32)


def dot_tn(a, b):
    return lax.dot_general(a, b, (((0,), (0,)), ((), ())), preferred_element_type=F32)


def tables(ids_ref):
    ids = [ids_ref[j : j + 1, :] for j in range(2)]
    lane = iota((N_E, TOK), 0)
    hits = [(i == lane).astype(F32) for i in ids]
    earlier = (iota((TOK, TOK), 0) < iota((TOK, TOK), 1)).astype(BF)
    rank = dot_nn((hits[0] + hits[1]).astype(BF), earlier)
    slot = iota((N_E * CAP, TOK), 0)
    out = []
    for j in range(2):
        place = jnp.sum(hits[j] * rank, axis=0, keepdims=True).astype(jnp.int32) + ids[j] * CAP
        out.append((slot == place).astype(F32))
    return out


def dispatch_kernel(ids_ref, gates_ref, tok_ref, cot_ref, out_ref):
    t0, t1 = tables(ids_ref)
    rows_in = dot_nn((t0 + t1).astype(BF), tok_ref[...]).astype(BF)
    rows_cot = jnp.zeros((N_E * CAP, LANE), F32)
    for j, table in enumerate((t0, t1)):
        gate = jnp.sum(table * gates_ref[j : j + 1, :], axis=1, keepdims=True)
        rows_cot = rows_cot + gate * dot_nn(table.astype(BF), cot_ref[...])
    rows_cot = rows_cot.astype(BF)
    for e in range(N_E):
        for q in range(N_Q):
            out_ref[e, q, 0:CAP] = rows_in[e * CAP : (e + 1) * CAP]
            out_ref[e, q, CAP : 2 * CAP] = rows_cot[e * CAP : (e + 1) * CAP]


def combine_kernel(ids_ref, gates_ref, back_ref, mixed_ref, grad_ref):
    t0, t1 = tables(ids_ref)
    total = back_ref[:, 0].astype(F32)
    for q in range(1, N_Q):
        total = total + back_ref[:, q].astype(F32)
    weighted = t0 * gates_ref[0:1, :] + t1 * gates_ref[1:2, :]
    for table, first, out_ref in ((weighted, 0, mixed_ref), (t0 + t1, CAP, grad_ref)):
        out_ref[...] = lax.dot_general(
            table,
            total[:, first : first + CAP].reshape(N_E * CAP, LANE),
            (((0,), (0,)), ((), ())),
            precision=lax.Precision.HIGHEST,
            preferred_element_type=F32,
        ).astype(BF)


def counts(marks_ref):
    upto = (iota((COLS, COLS), 0) <= iota((COLS, COLS), 1)).astype(BF)
    return dot_nn(marks_ref[...].astype(BF), upto)


def pick_row(values, row):
    return jnp.sum(jnp.where(iota(values.shape, 0) == row, values, 0.0), axis=0, keepdims=True)


def pack_kernel(where_ref, marks_ref, dense_ref, *outs):
    cum = counts(marks_ref)
    marks = marks_ref[...].astype(F32)
    col = iota((1, COLS), 1).astype(F32)
    dense = dense_ref[...]
    for k in range(N_X):
        expert = lax.rem(where_ref[0] + k, N_X) * 2 + where_ref[1]
        kept = jnp.where(pick_row(marks, expert) > 0.5, -1.0, col - pick_row(cum, expert))
        onehot = (iota((HALF, COLS), 0) == kept.astype(jnp.int32)).astype(BF)
        outs[k][...] = dot_nt(dense, onehot).astype(BF)


def order_of_units(where_ref, marks_ref):
    expert = where_ref[0] * 2 + where_ref[1]
    cum = pick_row(counts(marks_ref), expert)
    mark = pick_row(marks_ref[...].astype(F32), expert)
    col = iota((1, COLS), 1).astype(F32)
    source = jnp.where(mark > 0.5, HALF + cum - 1.0, col - cum).astype(jnp.int32)
    return (iota((COLS, COLS), 0) == source).astype(BF)


def slab_rows(rows_ref, z, first):
    return jnp.concatenate(
        [
            rows_ref[:, 0, z, q, first : first + CAP].reshape(ROWS, LANE)
            for q in range(N_Q)
        ],
        axis=1,
    )


def accumulate(step, accs, parts):
    @pl.when(step == 0)
    def _():
        for acc, part in zip(accs, parts):
            acc[...] = part

    @pl.when(step > 0)
    def _():
        for acc, part in zip(accs, parts):
            acc[...] += part


def expert_kernel(where_ref, rows_ref, fresh_ref, *refs):
    near, far, refs = refs[:N_X], refs[N_X : 2 * N_X], refs[2 * N_X :]
    hidden_ref, both_ref, out_ref, held, gate_acc, up_acc, down_acc = refs
    step = pl.program_id(0)
    z, other_z = where_ref[1], 1 - where_ref[1]

    for k in range(N_X):

        @pl.when(step == k)
        def _():
            for p in range(3):
                for side, (at, piece) in enumerate(((z, near[k][p]), (other_z, far[k][p]))):
                    held[k, p, side * SLAB : (side + 1) * SLAB, :] = jnp.concatenate(
                        [piece, fresh_ref[p, 0, at]], axis=1
                    )

    @pl.when(step < N_X)
    def _():
        rows_in = jnp.concatenate([slab_rows(rows_ref, z, 0), slab_rows(rows_ref, other_z, 0)], axis=1)
        rows_cot = jnp.concatenate(
            [slab_rows(rows_ref, z, CAP), slab_rows(rows_ref, other_z, CAP)], axis=1
        )
        parts = [
            dot_nn(r, held[step, p]) for p, r in enumerate((rows_in, rows_in, rows_cot))
        ]
        accumulate(step, (gate_acc, up_acc, down_acc), parts)

    @pl.when(step == N_X - 1)
    def _():
        gate, up, grad = gate_acc[...], up_acc[...], down_acc[...]
        sig = jax.nn.sigmoid(gate)
        act = gate * sig
        hidden_ref[...] = (act * up).astype(BF)
        both_ref[:, 0:COLS] = (grad * up * sig * (1.0 + gate * (1.0 - sig))).astype(BF)
        both_ref[:, COLS:] = (grad * act).astype(BF)

    @pl.when(step >= N_X)
    def _():
        k = step - N_X
        pair = jnp.concatenate([held[k, 0], held[k, 1]], axis=1)
        outs = dot_nt(hidden_ref[...], held[k, 2]).astype(BF)
        grads = dot_nt(both_ref[...], pair).astype(BF)
        for first, values in ((0, outs), (CAP, grads)):
            for side, at in enumerate((z, other_z)):
                for q in range(N_Q):
                    lane = side * SLAB + q * LANE
                    out_ref[:, 0, at, q, first : first + CAP] = values[
                        :, lane : lane + LANE
                    ].reshape(N_DP, CAP, LANE)


def update_kernel(where_ref, rows_ref, fresh_ref, *refs):
    near, far, refs = refs[:N_X], refs[N_X : 2 * N_X], refs[2 * N_X :]
    hidden_ref, both_ref, marks_ref, new_ref, order, held = refs
    step = pl.program_id(0)

    @pl.when(step == 0)
    def _():
        order[...] = order_of_units(where_ref, marks_ref)

    for k in range(N_X):

        @pl.when(step == k)
        def _():
            for p in range(3):
                held[p, 0] = near[k][p]
                held[p, 1] = far[k][p]

    for side, z in enumerate((where_ref[1], 1 - where_ref[1])):
        pair = dot_tn(slab_rows(rows_ref, z, 0), both_ref[...])
        down = dot_tn(slab_rows(rows_ref, z, CAP), hidden_ref[...])
        for p, g in enumerate((pair[:, 0:COLS], pair[:, COLS:], down)):
            w = jnp.concatenate([held[p, side], fresh_ref[p, 0, z]], axis=1).astype(F32)
            new = w * (1.0 - 0.0003) - 0.003 * (g / (jnp.abs(g) + 0.1))
            new_ref[p, 0, z] = dot_nn(new.astype(BF), order[...]).astype(BF)


def call(kernel, outs, prefetch=0, scratch=(), **kw):
    if "grid" in kw:
        kw = dict(
            grid_spec=pltpu.PrefetchScalarGridSpec(
                num_scalar_prefetch=prefetch, scratch_shapes=list(scratch), **kw
            )
        )
    return pl.pallas_call(
        kernel,
        out_shape=outs,
        compiler_params=pltpu.CompilerParams(vmem_limit_bytes=VMEM_CAP),
        cost_estimate=pl.CostEstimate(flops=COST, bytes_accessed=COST, transcendentals=0),
        **kw,
    )


COST = 1024


def sds(shape, dtype=BF):
    return jax.ShapeDtypeStruct(shape, dtype)


SMEM = pl.BlockSpec(memory_space=pltpu.SMEM)
VIEW = (N_X, 2, N_Q, 2 * CAP, LANE)


def block_x(k, w):
    return lax.rem(w[0] + N_X - k, N_X)


def front_step(i):
    return jnp.minimum(i, N_X - 1)


def back_step(i):
    return jnp.maximum(i - N_X, 0)


def rows_spec(step):
    return pl.BlockSpec(
        (N_DP, 1) + VIEW[1:], lambda i, w: (0, block_x(step(i), w), 0, 0, 0, 0)
    )


def whole_spec(shape):
    return pl.BlockSpec(shape, lambda i, w: (0,) * len(shape))


FRESH_SPEC = pl.BlockSpec(
    (3, 1, 2, SLAB, HALF), lambda i, w: (0, block_x(front_step(i), w), 0, 0, 0)
)


def after(values, *first):
    return lax.optimization_barrier((values, first))[0]


def on_device(tokens, cotangent, gates, expert_ids, dense_ffn, redrawn, redraw):
    expert = lax.axis_index("expert")
    x, z = expert // 2, expert % 2
    where = jnp.stack([x, z]).astype(jnp.int32)

    def along_x(piece, k):
        return lax.ppermute(
            piece, "expert", [(e, (e // 2 + k) % N_X * 2 + e % 2) for e in range(N_E)]
        )

    def other_side(slab):
        return lax.ppermute(slab, "expert", [(e, e ^ 1) for e in range(N_E)])

    def exchange(rows):
        return lax.all_to_all(rows, ("expert", "mp"), split_axis=0, concat_axis=0, tiled=True)

    def pack(slab):
        rows = slab.shape[0]
        return call(
            pack_kernel,
            [sds((rows, HALF))] * N_X,
            in_specs=[SMEM, pl.BlockSpec(), pl.BlockSpec()],
        )(where, redrawn, slab)

    def to_holders(packed):
        return [packed[0]] + [along_x(packed[k], k) for k in range(1, N_X)]

    ids, weights = expert_ids.T, gates.T
    slots = call(dispatch_kernel, sds((N_E, N_Q, 2 * CAP, LANE)))(ids, weights, tokens, cotangent)
    mine = exchange(slots.reshape(2 * PIECE, LANE))

    rows = lax.all_gather(mine, "dp", axis=0, tiled=True).reshape((N_DP,) + VIEW)
    dense = dense_ffn.reshape(3 * SLAB, COLS)
    mine, dense, near = lax.optimization_barrier((mine, dense, pack(dense)))
    near = to_holders(near)
    far = to_holders(pack(other_side(dense)))
    pieces = [p.reshape(3, SLAB, HALF) for p in near + far]
    piece_specs = [whole_spec(p.shape) for p in pieces]
    fresh = redraw.reshape(3, N_X, 2, SLAB, HALF)

    acts = [sds((ROWS, COLS)), sds((ROWS, 2 * COLS))]
    act_specs = [whole_spec(a.shape) for a in acts]
    hidden, both, sums = call(
        expert_kernel,
        acts + [sds((N_DP,) + VIEW)],
        prefetch=1,
        scratch=[pltpu.VMEM((N_X, 3, 2 * SLAB, COLS), BF)] + [pltpu.VMEM((ROWS, COLS), F32)] * 3,
        grid=(2 * N_X,),
        in_specs=[rows_spec(front_step), FRESH_SPEC] + piece_specs,
        out_specs=act_specs + [rows_spec(back_step)],
    )(where, rows, fresh, *pieces)

    total = lax.psum_scatter(
        sums.reshape(N_DP * 2 * PIECE, LANE), "dp", scatter_dimension=0, tiled=True
    )
    new_weights = call(
        update_kernel,
        sds((3, N_X, 2, SLAB, COLS)),
        prefetch=1,
        scratch=[pltpu.VMEM((COLS, COLS), BF), pltpu.VMEM((3, 2, SLAB, HALF), BF)],
        grid=(N_X,),
        in_specs=[rows_spec(front_step), FRESH_SPEC]
        + piece_specs
        + act_specs
        + [whole_spec((N_E, COLS))],
        out_specs=pl.BlockSpec(
            (3, 1, 2, SLAB, COLS), lambda i, w: (0, block_x(i, w), 0, 0, 0)
        ),
    )(where, rows, fresh, *pieces, hidden, both, redrawn)
    back = exchange(total).reshape(N_E, N_Q, 2 * CAP, LANE)
    mixed, token_grad = call(combine_kernel, [sds((TOK, LANE))] * 2)(ids, weights, back)
    return (mixed, token_grad, new_weights.reshape(1, 3, N_E * SLAB, COLS))


def solution(mesh):
    return jax.shard_map(
        on_device,
        mesh=mesh,
        in_specs=(
            P("dp", ("expert", "mp")),
            P("dp", ("expert", "mp")),
            P("dp", None),
            P("dp", None),
            P(None, "expert", ("dp", "mp")),
            P(None, ("dp", "mp")),
            P("expert", None, None, ("dp", "mp")),
        ),
        out_specs=(
            P("dp", ("expert", "mp")),
            P("dp", ("expert", "mp")),
            P("expert", None, None, ("dp", "mp")),
        ),
        check_vma=False,
    )
```

```python
import jax
import jax.numpy as jnp
from jax import lax
from jax.experimental import pallas as pl
from jax.experimental.pallas import tpu as pltpu
from jax.sharding import PartitionSpec as P

BF = jnp.bfloat16
F32 = jnp.float32
CAP = 48
N_E = 8
N_DP = 8
N_X = 4
LANE = 128
COLS = 256
HALF = 128
SLAB = 512
TOK = 128
ROWS = N_DP * CAP
VMEM_CAP = 60 * 1024 * 1024
N_Y = 4
N_Q = 4
PIECE = N_E * N_Q * CAP


def iota(shape, dim):
    return lax.broadcasted_iota(jnp.int32, shape, dim)


def dot_nn(a, b):
    return lax.dot_general(a, b, (((1,), (0,)), ((), ())), preferred_element_type=F32)


def dot_nt(a, b):
    return lax.dot_general(a, b, (((1,), (1,)), ((), ())), preferred_element_type=F32)


def dot_tn(a, b):
    return lax.dot_general(a, b, (((0,), (0,)), ((), ())), preferred_element_type=F32)


def tables(ids_ref):
    ids = [ids_ref[j : j + 1, :] for j in range(2)]
    lane = iota((N_E, TOK), 0)
    hits = [(i == lane).astype(F32) for i in ids]
    earlier = (iota((TOK, TOK), 0) < iota((TOK, TOK), 1)).astype(BF)
    rank = dot_nn((hits[0] + hits[1]).astype(BF), earlier)
    slot = iota((N_E * CAP, TOK), 0)
    out = []
    for j in range(2):
        place = jnp.sum(hits[j] * rank, axis=0, keepdims=True).astype(jnp.int32) + ids[j] * CAP
        out.append((slot == place).astype(F32))
    return out


def dispatch_kernel(ids_ref, gates_ref, tok_ref, cot_ref, out_ref):
    t0, t1 = tables(ids_ref)
    rows_in = dot_nn((t0 + t1).astype(BF), tok_ref[...]).astype(BF)
    rows_cot = jnp.zeros((N_E * CAP, LANE), F32)
    for j, table in enumerate((t0, t1)):
        gate = jnp.sum(table * gates_ref[j : j + 1, :], axis=1, keepdims=True)
        rows_cot = rows_cot + gate * dot_nn(table.astype(BF), cot_ref[...])
    rows_cot = rows_cot.astype(BF)
    for e in range(N_E):
        for q in range(N_Q):
            out_ref[e, q, 0:CAP] = rows_in[e * CAP : (e + 1) * CAP]
            out_ref[e, q, CAP : 2 * CAP] = rows_cot[e * CAP : (e + 1) * CAP]


def combine_kernel(ids_ref, gates_ref, back_ref, mixed_ref, grad_ref):
    t0, t1 = tables(ids_ref)
    total = back_ref[:, 0].astype(F32)
    for q in range(1, N_Q):
        total = total + back_ref[:, q].astype(F32)
    weighted = t0 * gates_ref[0:1, :] + t1 * gates_ref[1:2, :]
    for table, first, out_ref in ((weighted, 0, mixed_ref), (t0 + t1, CAP, grad_ref)):
        out_ref[...] = lax.dot_general(
            table,
            total[:, first : first + CAP].reshape(N_E * CAP, LANE),
            (((0,), (0,)), ((), ())),
            precision=lax.Precision.HIGHEST,
            preferred_element_type=F32,
        ).astype(BF)


def counts(marks_ref):
    upto = (iota((COLS, COLS), 0) <= iota((COLS, COLS), 1)).astype(BF)
    return dot_nn(marks_ref[...].astype(BF), upto)


def pick_row(values, row):
    return jnp.sum(jnp.where(iota(values.shape, 0) == row, values, 0.0), axis=0, keepdims=True)


def pack_kernel(where_ref, marks_ref, dense_ref, *outs):
    cum = counts(marks_ref)
    marks = marks_ref[...].astype(F32)
    col = iota((1, COLS), 1).astype(F32)
    dense = dense_ref[...]
    for k in range(N_X):
        expert = lax.rem(where_ref[0] + k, N_X) * 2 + where_ref[1]
        kept = jnp.where(pick_row(marks, expert) > 0.5, -1.0, col - pick_row(cum, expert))
        onehot = (iota((HALF, COLS), 0) == kept.astype(jnp.int32)).astype(BF)
        outs[k][...] = dot_nt(dense, onehot).astype(BF)


def order_of_units(where_ref, marks_ref):
    expert = where_ref[0] * 2 + where_ref[1]
    cum = pick_row(counts(marks_ref), expert)
    mark = pick_row(marks_ref[...].astype(F32), expert)
    col = iota((1, COLS), 1).astype(F32)
    source = jnp.where(mark > 0.5, HALF + cum - 1.0, col - cum).astype(jnp.int32)
    return (iota((COLS, COLS), 0) == source).astype(BF)


def slab_rows(rows_ref, z, first):
    return jnp.concatenate(
        [
            rows_ref[:, 0, z, q, first : first + CAP].reshape(ROWS, LANE)
            for q in range(N_Q)
        ],
        axis=1,
    )


def accumulate(step, accs, parts):
    @pl.when(step == 0)
    def _():
        for acc, part in zip(accs, parts):
            acc[...] = part

    @pl.when(step > 0)
    def _():
        for acc, part in zip(accs, parts):
            acc[...] += part


def far_piece(far, p, k):
    return far[k][0] if p == 0 else far[N_X + k][p - 1]


def expert_kernel(where_ref, rows_ref, fresh_ref, *refs):
    near, far, refs = refs[:N_X], refs[N_X : 3 * N_X], refs[3 * N_X :]
    hidden_ref, both_ref, out_ref, held, gate_acc, up_acc, down_acc = refs
    step = pl.program_id(0)
    z, other_z = where_ref[1], 1 - where_ref[1]

    for k in range(N_X):

        @pl.when(step == k)
        def _():
            for p in range(3):
                for side, (at, piece) in enumerate(((z, near[k][p]), (other_z, far_piece(far, p, k)))):
                    held[k, p, side * SLAB : (side + 1) * SLAB, :] = jnp.concatenate(
                        [piece, fresh_ref[p, 0, at]], axis=1
                    )

    @pl.when(step < N_X)
    def _():
        rows_in = jnp.concatenate([slab_rows(rows_ref, z, 0), slab_rows(rows_ref, other_z, 0)], axis=1)
        rows_cot = jnp.concatenate(
            [slab_rows(rows_ref, z, CAP), slab_rows(rows_ref, other_z, CAP)], axis=1
        )
        parts = [
            dot_nn(r, held[step, p]) for p, r in enumerate((rows_in, rows_in, rows_cot))
        ]
        accumulate(step, (gate_acc, up_acc, down_acc), parts)

    @pl.when(step == N_X - 1)
    def _():
        gate, up, grad = gate_acc[...], up_acc[...], down_acc[...]
        sig = jax.nn.sigmoid(gate)
        act = gate * sig
        hidden_ref[...] = (act * up).astype(BF)
        both_ref[:, 0:COLS] = (grad * up * sig * (1.0 + gate * (1.0 - sig))).astype(BF)
        both_ref[:, COLS:] = (grad * act).astype(BF)

    @pl.when(step >= N_X)
    def _():
        k = step - N_X
        pair = jnp.concatenate([held[k, 0], held[k, 1]], axis=1)
        outs = dot_nt(hidden_ref[...], held[k, 2]).astype(BF)
        grads = dot_nt(both_ref[...], pair).astype(BF)
        for first, values in ((0, outs), (CAP, grads)):
            for side, at in enumerate((z, other_z)):
                for q in range(N_Q):
                    lane = side * SLAB + q * LANE
                    out_ref[:, 0, at, q, first : first + CAP] = values[
                        :, lane : lane + LANE
                    ].reshape(N_DP, CAP, LANE)


def update_kernel(where_ref, rows_ref, fresh_ref, *refs):
    near, far, refs = refs[:N_X], refs[N_X : 3 * N_X], refs[3 * N_X :]
    hidden_ref, both_ref, marks_ref, new_ref, order, held = refs
    step = pl.program_id(0)

    @pl.when(step == 0)
    def _():
        order[...] = order_of_units(where_ref, marks_ref)

    for k in range(N_X):

        @pl.when(step == k)
        def _():
            for p in range(3):
                held[p, 0] = near[k][p]
                held[p, 1] = far_piece(far, p, k)

    for side, z in enumerate((where_ref[1], 1 - where_ref[1])):
        pair = dot_tn(slab_rows(rows_ref, z, 0), both_ref[...])
        down = dot_tn(slab_rows(rows_ref, z, CAP), hidden_ref[...])
        for p, g in enumerate((pair[:, 0:COLS], pair[:, COLS:], down)):
            w = jnp.concatenate([held[p, side], fresh_ref[p, 0, z]], axis=1).astype(F32)
            new = w * (1.0 - 0.0003) - 0.003 * (g / (jnp.abs(g) + 0.1))
            new_ref[p, 0, z] = dot_nn(new.astype(BF), order[...]).astype(BF)


def call(kernel, outs, prefetch=0, scratch=(), **kw):
    if "grid" in kw:
        kw = dict(
            grid_spec=pltpu.PrefetchScalarGridSpec(
                num_scalar_prefetch=prefetch, scratch_shapes=list(scratch), **kw
            )
        )
    return pl.pallas_call(
        kernel,
        out_shape=outs,
        compiler_params=pltpu.CompilerParams(vmem_limit_bytes=VMEM_CAP),
        cost_estimate=pl.CostEstimate(flops=COST, bytes_accessed=COST, transcendentals=0),
        **kw,
    )


COST = 1024


def sds(shape, dtype=BF):
    return jax.ShapeDtypeStruct(shape, dtype)


SMEM = pl.BlockSpec(memory_space=pltpu.SMEM)
VIEW = (N_X, 2, N_Q, 2 * CAP, LANE)


def block_x(k, w):
    return lax.rem(w[0] + N_X - k, N_X)


def front_step(i):
    return jnp.minimum(i, N_X - 1)


def back_step(i):
    return jnp.maximum(i - N_X, 0)


def rows_spec(step):
    return pl.BlockSpec(
        (N_DP, 1) + VIEW[1:], lambda i, w: (0, block_x(step(i), w), 0, 0, 0, 0)
    )


def whole_spec(shape):
    return pl.BlockSpec(shape, lambda i, w: (0,) * len(shape))


FRESH_SPEC = pl.BlockSpec(
    (3, 1, 2, SLAB, HALF), lambda i, w: (0, block_x(front_step(i), w), 0, 0, 0)
)


def after(values, *first):
    return lax.optimization_barrier((values, first))[0]


def on_device(tokens, cotangent, gates, expert_ids, dense_ffn, redrawn, redraw):
    expert = lax.axis_index("expert")
    x, z = expert // 2, expert % 2
    where = jnp.stack([x, z]).astype(jnp.int32)

    def along_x(piece, k):
        return lax.ppermute(
            piece, "expert", [(e, (e // 2 + k) % N_X * 2 + e % 2) for e in range(N_E)]
        )

    def other_side(slab):
        return lax.ppermute(slab, "expert", [(e, e ^ 1) for e in range(N_E)])

    def exchange(rows):
        return lax.all_to_all(rows, ("expert", "mp"), split_axis=0, concat_axis=0, tiled=True)

    def pack(slab):
        rows = slab.shape[0]
        return call(
            pack_kernel,
            [sds((rows, HALF))] * N_X,
            in_specs=[SMEM, pl.BlockSpec(), pl.BlockSpec()],
        )(where, redrawn, slab)

    def to_holders(packed):
        return [packed[0]] + [along_x(packed[k], k) for k in range(1, N_X)]

    ids, weights = expert_ids.T, gates.T
    slots = call(dispatch_kernel, sds((N_E, N_Q, 2 * CAP, LANE)))(ids, weights, tokens, cotangent)
    near = pack(dense_ffn.reshape(3 * SLAB, COLS))
    mine = exchange(after(slots.reshape(2 * PIECE, LANE), *near))

    near = to_holders(near)
    rest = dense_ffn[1:].reshape(2 * SLAB, COLS)
    mine, near, gate, rest = lax.optimization_barrier(
        (mine, near, other_side(dense_ffn[0]), rest)
    )
    rows = lax.all_gather(mine, "dp", axis=0, tiled=True).reshape((N_DP,) + VIEW)
    rest = other_side(rest)
    gate, rest = lax.optimization_barrier((to_holders(pack(gate)), rest))
    rest = to_holders(pack(rest))
    pieces = [
        p.reshape(n, SLAB, HALF) for n, part in ((3, near), (1, gate), (2, rest)) for p in part
    ]
    piece_specs = [whole_spec(p.shape) for p in pieces]
    fresh = redraw.reshape(3, N_X, 2, SLAB, HALF)

    acts = [sds((ROWS, COLS)), sds((ROWS, 2 * COLS))]
    act_specs = [whole_spec(a.shape) for a in acts]
    hidden, both, sums = call(
        expert_kernel,
        acts + [sds((N_DP,) + VIEW)],
        prefetch=1,
        scratch=[pltpu.VMEM((N_X, 3, 2 * SLAB, COLS), BF)] + [pltpu.VMEM((ROWS, COLS), F32)] * 3,
        grid=(2 * N_X,),
        in_specs=[rows_spec(front_step), FRESH_SPEC] + piece_specs,
        out_specs=act_specs + [rows_spec(back_step)],
    )(where, rows, fresh, *pieces)

    total = lax.psum_scatter(
        sums.reshape(N_DP * 2 * PIECE, LANE), "dp", scatter_dimension=0, tiled=True
    )
    new_weights = call(
        update_kernel,
        sds((3, N_X, 2, SLAB, COLS)),
        prefetch=1,
        scratch=[pltpu.VMEM((COLS, COLS), BF), pltpu.VMEM((3, 2, SLAB, HALF), BF)],
        grid=(N_X,),
        in_specs=[rows_spec(front_step), FRESH_SPEC]
        + piece_specs
        + act_specs
        + [whole_spec((N_E, COLS))],
        out_specs=pl.BlockSpec(
            (3, 1, 2, SLAB, COLS), lambda i, w: (0, block_x(i, w), 0, 0, 0)
        ),
    )(where, rows, fresh, *pieces, hidden, both, redrawn)
    back = exchange(total).reshape(N_E, N_Q, 2 * CAP, LANE)
    mixed, token_grad = call(combine_kernel, [sds((TOK, LANE))] * 2)(ids, weights, back)
    return (mixed, token_grad, new_weights.reshape(1, 3, N_E * SLAB, COLS))


def solution(mesh):
    return jax.shard_map(
        on_device,
        mesh=mesh,
        in_specs=(
            P("dp", ("expert", "mp")),
            P("dp", ("expert", "mp")),
            P("dp", None),
            P("dp", None),
            P(None, "expert", ("dp", "mp")),
            P(None, ("dp", "mp")),
            P("expert", None, None, ("dp", "mp")),
        ),
        out_specs=(
            P("dp", ("expert", "mp")),
            P("dp", ("expert", "mp")),
            P("expert", None, None, ("dp", "mp")),
        ),
        check_vma=False,
    )
```

```python
import jax
import jax.numpy as jnp
from jax import lax
from jax.experimental import pallas as pl
from jax.experimental.pallas import tpu as pltpu
from jax.sharding import PartitionSpec as P

BF = jnp.bfloat16
F32 = jnp.float32
CAP = 48
N_E = 8
N_DP = 8
N_X = 4
LANE = 128
COLS = 256
HALF = 128
SLAB = 512
TOK = 128
ROWS = N_DP * CAP
VMEM_CAP = 60 * 1024 * 1024
N_Y = 4
N_Q = 4
PIECE = N_E * N_Q * CAP


def iota(shape, dim):
    return lax.broadcasted_iota(jnp.int32, shape, dim)


def dot_nn(a, b):
    return lax.dot_general(a, b, (((1,), (0,)), ((), ())), preferred_element_type=F32)


def dot_nt(a, b):
    return lax.dot_general(a, b, (((1,), (1,)), ((), ())), preferred_element_type=F32)


def dot_tn(a, b):
    return lax.dot_general(a, b, (((0,), (0,)), ((), ())), preferred_element_type=F32)


def tables(ids_ref):
    ids = [ids_ref[j : j + 1, :] for j in range(2)]
    lane = iota((N_E, TOK), 0)
    hits = [(i == lane).astype(F32) for i in ids]
    earlier = (iota((TOK, TOK), 0) < iota((TOK, TOK), 1)).astype(BF)
    rank = dot_nn((hits[0] + hits[1]).astype(BF), earlier)
    slot = iota((N_E * CAP, TOK), 0)
    out = []
    for j in range(2):
        place = jnp.sum(hits[j] * rank, axis=0, keepdims=True).astype(jnp.int32) + ids[j] * CAP
        out.append((slot == place).astype(F32))
    return out


def dispatch_kernel(ids_ref, gates_ref, tok_ref, cot_ref, out_ref):
    t0, t1 = tables(ids_ref)
    rows_in = dot_nn((t0 + t1).astype(BF), tok_ref[...]).astype(BF)
    rows_cot = jnp.zeros((N_E * CAP, LANE), F32)
    for j, table in enumerate((t0, t1)):
        gate = jnp.sum(table * gates_ref[j : j + 1, :], axis=1, keepdims=True)
        rows_cot = rows_cot + gate * dot_nn(table.astype(BF), cot_ref[...])
    rows_cot = rows_cot.astype(BF)
    for e in range(N_E):
        for q in range(N_Q):
            out_ref[e, q, 0:CAP] = rows_in[e * CAP : (e + 1) * CAP]
            out_ref[e, q, CAP : 2 * CAP] = rows_cot[e * CAP : (e + 1) * CAP]


def combine_kernel(ids_ref, gates_ref, back_ref, mixed_ref, grad_ref):
    t0, t1 = tables(ids_ref)
    total = back_ref[:, 0].astype(F32)
    for q in range(1, N_Q):
        total = total + back_ref[:, q].astype(F32)
    weighted = t0 * gates_ref[0:1, :] + t1 * gates_ref[1:2, :]
    for table, first, out_ref in ((weighted, 0, mixed_ref), (t0 + t1, CAP, grad_ref)):
        out_ref[...] = lax.dot_general(
            table,
            total[:, first : first + CAP].reshape(N_E * CAP, LANE),
            (((0,), (0,)), ((), ())),
            precision=lax.Precision.HIGHEST,
            preferred_element_type=F32,
        ).astype(BF)


def counts(marks_ref):
    upto = (iota((COLS, COLS), 0) <= iota((COLS, COLS), 1)).astype(BF)
    return dot_nn(marks_ref[...].astype(BF), upto)


def pick_row(values, row):
    return jnp.sum(jnp.where(iota(values.shape, 0) == row, values, 0.0), axis=0, keepdims=True)


def pack_kernel(where_ref, marks_ref, dense_ref, *outs):
    cum = counts(marks_ref)
    marks = marks_ref[...].astype(F32)
    col = iota((1, COLS), 1).astype(F32)
    dense = dense_ref[...]
    for k in range(N_X):
        expert = lax.rem(where_ref[0] + k, N_X) * 2 + where_ref[1]
        kept = jnp.where(pick_row(marks, expert) > 0.5, -1.0, col - pick_row(cum, expert))
        onehot = (iota((HALF, COLS), 0) == kept.astype(jnp.int32)).astype(BF)
        outs[k][...] = dot_nt(dense, onehot).astype(BF)


def order_of_units(where_ref, marks_ref):
    expert = where_ref[0] * 2 + where_ref[1]
    cum = pick_row(counts(marks_ref), expert)
    mark = pick_row(marks_ref[...].astype(F32), expert)
    col = iota((1, COLS), 1).astype(F32)
    source = jnp.where(mark > 0.5, HALF + cum - 1.0, col - cum).astype(jnp.int32)
    return (iota((COLS, COLS), 0) == source).astype(BF)


def slab_rows(rows_ref, z, first):
    return jnp.concatenate(
        [
            rows_ref[:, 0, z, q, first : first + CAP].reshape(ROWS, LANE)
            for q in range(N_Q)
        ],
        axis=1,
    )


def accumulate(step, accs, parts):
    @pl.when(step == 0)
    def _():
        for acc, part in zip(accs, parts):
            acc[...] = part

    @pl.when(step > 0)
    def _():
        for acc, part in zip(accs, parts):
            acc[...] += part


def far_piece(far, p, k):
    return far[p * N_X + k][...]


def expert_kernel(where_ref, rows_ref, fresh_ref, *refs):
    near, far, refs = refs[:N_X], refs[N_X : 4 * N_X], refs[4 * N_X :]
    hidden_ref, both_ref, out_ref, held, gate_acc, up_acc, down_acc = refs
    step = pl.program_id(0)
    z, other_z = where_ref[1], 1 - where_ref[1]

    for k in range(N_X):

        @pl.when(step == k)
        def _():
            for p in range(3):
                for side, (at, piece) in enumerate(((z, near[k][p]), (other_z, far_piece(far, p, k)))):
                    held[k, p, side * SLAB : (side + 1) * SLAB, :] = jnp.concatenate(
                        [piece, fresh_ref[p, 0, at]], axis=1
                    )

    @pl.when(step < N_X)
    def _():
        rows_in = jnp.concatenate([slab_rows(rows_ref, z, 0), slab_rows(rows_ref, other_z, 0)], axis=1)
        rows_cot = jnp.concatenate(
            [slab_rows(rows_ref, z, CAP), slab_rows(rows_ref, other_z, CAP)], axis=1
        )
        parts = [
            dot_nn(r, held[step, p]) for p, r in enumerate((rows_in, rows_in, rows_cot))
        ]
        accumulate(step, (gate_acc, up_acc, down_acc), parts)

    @pl.when(step == N_X - 1)
    def _():
        gate, up, grad = gate_acc[...], up_acc[...], down_acc[...]
        sig = jax.nn.sigmoid(gate)
        act = gate * sig
        hidden_ref[...] = (act * up).astype(BF)
        both_ref[:, 0:COLS] = (grad * up * sig * (1.0 + gate * (1.0 - sig))).astype(BF)
        both_ref[:, COLS:] = (grad * act).astype(BF)

    @pl.when(step >= N_X)
    def _():
        k = step - N_X
        pair = jnp.concatenate([held[k, 0], held[k, 1]], axis=1)
        outs = dot_nt(hidden_ref[...], held[k, 2]).astype(BF)
        grads = dot_nt(both_ref[...], pair).astype(BF)
        for first, values in ((0, outs), (CAP, grads)):
            for side, at in enumerate((z, other_z)):
                for q in range(N_Q):
                    lane = side * SLAB + q * LANE
                    out_ref[:, 0, at, q, first : first + CAP] = values[
                        :, lane : lane + LANE
                    ].reshape(N_DP, CAP, LANE)


def update_kernel(where_ref, rows_ref, fresh_ref, *refs):
    near, far, refs = refs[:N_X], refs[N_X : 4 * N_X], refs[4 * N_X :]
    hidden_ref, both_ref, marks_ref, new_ref, order, held = refs
    step = pl.program_id(0)

    @pl.when(step == 0)
    def _():
        order[...] = order_of_units(where_ref, marks_ref)

    for k in range(N_X):

        @pl.when(step == k)
        def _():
            for p in range(3):
                held[p, 0] = near[k][p]
                held[p, 1] = far_piece(far, p, k)

    for side, z in enumerate((where_ref[1], 1 - where_ref[1])):
        pair = dot_tn(slab_rows(rows_ref, z, 0), both_ref[...])
        down = dot_tn(slab_rows(rows_ref, z, CAP), hidden_ref[...])
        for p, g in enumerate((pair[:, 0:COLS], pair[:, COLS:], down)):
            w = jnp.concatenate([held[p, side], fresh_ref[p, 0, z]], axis=1).astype(F32)
            new = w * (1.0 - 0.0003) - 0.003 * (g / (jnp.abs(g) + 0.1))
            new_ref[p, 0, z] = dot_nn(new.astype(BF), order[...]).astype(BF)


def call(kernel, outs, prefetch=0, scratch=(), **kw):
    if "grid" in kw:
        kw = dict(
            grid_spec=pltpu.PrefetchScalarGridSpec(
                num_scalar_prefetch=prefetch, scratch_shapes=list(scratch), **kw
            )
        )
    return pl.pallas_call(
        kernel,
        out_shape=outs,
        compiler_params=pltpu.CompilerParams(vmem_limit_bytes=VMEM_CAP),
        cost_estimate=pl.CostEstimate(flops=COST, bytes_accessed=COST, transcendentals=0),
        **kw,
    )


COST = 1024


def sds(shape, dtype=BF):
    return jax.ShapeDtypeStruct(shape, dtype)


SMEM = pl.BlockSpec(memory_space=pltpu.SMEM)
VIEW = (N_X, 2, N_Q, 2 * CAP, LANE)


def block_x(k, w):
    return lax.rem(w[0] + N_X - k, N_X)


def front_step(i):
    return jnp.minimum(i, N_X - 1)


def back_step(i):
    return jnp.maximum(i - N_X, 0)


def rows_spec(step):
    return pl.BlockSpec(
        (N_DP, 1) + VIEW[1:], lambda i, w: (0, block_x(step(i), w), 0, 0, 0, 0)
    )


def whole_spec(shape):
    return pl.BlockSpec(shape, lambda i, w: (0,) * len(shape))


FRESH_SPEC = pl.BlockSpec(
    (3, 1, 2, SLAB, HALF), lambda i, w: (0, block_x(front_step(i), w), 0, 0, 0)
)


def after(values, *first):
    return lax.optimization_barrier((values, first))[0]


def on_device(tokens, cotangent, gates, expert_ids, dense_ffn, redrawn, redraw):
    expert = lax.axis_index("expert")
    x, z = expert // 2, expert % 2
    where = jnp.stack([x, z]).astype(jnp.int32)

    def along_x(piece, k):
        return lax.ppermute(
            piece, "expert", [(e, (e // 2 + k) % N_X * 2 + e % 2) for e in range(N_E)]
        )

    def other_side(slab):
        return lax.ppermute(slab, "expert", [(e, e ^ 1) for e in range(N_E)])

    def exchange(rows):
        return lax.all_to_all(rows, ("expert", "mp"), split_axis=0, concat_axis=0, tiled=True)

    def pack(slab):
        rows = slab.shape[0]
        return call(
            pack_kernel,
            [sds((rows, HALF))] * N_X,
            in_specs=[SMEM, pl.BlockSpec(), pl.BlockSpec()],
        )(where, redrawn, slab)

    def to_holders(packed):
        return [packed[0]] + [along_x(packed[k], k) for k in range(1, N_X)]

    ids, weights = expert_ids.T, gates.T
    slots = call(dispatch_kernel, sds((N_E, N_Q, 2 * CAP, LANE)))(ids, weights, tokens, cotangent)
    parts = [dense_ffn[p] for p in range(3)]
    near = pack(dense_ffn.reshape(3 * SLAB, COLS))
    slots, parts = lax.optimization_barrier((slots, parts))
    mine = exchange(slots.reshape(2 * PIECE, LANE))

    gate = other_side(parts[0])
    near = to_holders(near)
    mine, near, gate, parts = lax.optimization_barrier((mine, near, gate, parts))
    rows = lax.all_gather(mine, "dp", axis=0, tiled=True).reshape((N_DP,) + VIEW)
    up, down = other_side(parts[1]), other_side(parts[2])
    gate, up = lax.optimization_barrier((to_holders(pack(gate)), up))
    up, down = lax.optimization_barrier((to_holders(pack(up)), down))
    pieces = [p.reshape(3, SLAB, HALF) for p in near] + gate + up + to_holders(pack(down))
    piece_specs = [whole_spec(p.shape) for p in pieces]
    fresh = redraw.reshape(3, N_X, 2, SLAB, HALF)

    acts = [sds((ROWS, COLS)), sds((ROWS, 2 * COLS))]
    act_specs = [whole_spec(a.shape) for a in acts]
    hidden, both, sums = call(
        expert_kernel,
        acts + [sds((N_DP,) + VIEW)],
        prefetch=1,
        scratch=[pltpu.VMEM((N_X, 3, 2 * SLAB, COLS), BF)] + [pltpu.VMEM((ROWS, COLS), F32)] * 3,
        grid=(2 * N_X,),
        in_specs=[rows_spec(front_step), FRESH_SPEC] + piece_specs,
        out_specs=act_specs + [rows_spec(back_step)],
    )(where, rows, fresh, *pieces)

    total = lax.psum_scatter(
        sums.reshape(N_DP * 2 * PIECE, LANE), "dp", scatter_dimension=0, tiled=True
    )
    new_weights = call(
        update_kernel,
        sds((3, N_X, 2, SLAB, COLS)),
        prefetch=1,
        scratch=[pltpu.VMEM((COLS, COLS), BF), pltpu.VMEM((3, 2, SLAB, HALF), BF)],
        grid=(N_X,),
        in_specs=[rows_spec(front_step), FRESH_SPEC]
        + piece_specs
        + act_specs
        + [whole_spec((N_E, COLS))],
        out_specs=pl.BlockSpec(
            (3, 1, 2, SLAB, COLS), lambda i, w: (0, block_x(i, w), 0, 0, 0)
        ),
    )(where, rows, fresh, *pieces, hidden, both, redrawn)
    back = exchange(total).reshape(N_E, N_Q, 2 * CAP, LANE)
    mixed, token_grad = call(combine_kernel, [sds((TOK, LANE))] * 2)(ids, weights, back)
    return (mixed, token_grad, new_weights.reshape(1, 3, N_E * SLAB, COLS))


def solution(mesh):
    return jax.shard_map(
        on_device,
        mesh=mesh,
        in_specs=(
            P("dp", ("expert", "mp")),
            P("dp", ("expert", "mp")),
            P("dp", None),
            P("dp", None),
            P(None, "expert", ("dp", "mp")),
            P(None, ("dp", "mp")),
            P("expert", None, None, ("dp", "mp")),
        ),
        out_specs=(
            P("dp", ("expert", "mp")),
            P("dp", ("expert", "mp")),
            P("expert", None, None, ("dp", "mp")),
        ),
        check_vma=False,
    )
```

```python
import jax
import jax.numpy as jnp
from jax import lax
from jax.experimental import pallas as pl
from jax.experimental.pallas import tpu as pltpu
from jax.sharding import PartitionSpec as P

BF = jnp.bfloat16
F32 = jnp.float32
CAP = 48
N_E = 8
N_DP = 8
N_X = 4
LANE = 128
COLS = 256
HALF = 128
SLAB = 512
TOK = 128
ROWS = N_DP * CAP
VMEM_CAP = 60 * 1024 * 1024
N_Y = 4
N_Q = 4
PIECE = N_E * N_Q * CAP


def iota(shape, dim):
    return lax.broadcasted_iota(jnp.int32, shape, dim)


def dot_nn(a, b):
    return lax.dot_general(a, b, (((1,), (0,)), ((), ())), preferred_element_type=F32)


def dot_nt(a, b):
    return lax.dot_general(a, b, (((1,), (1,)), ((), ())), preferred_element_type=F32)


def dot_tn(a, b):
    return lax.dot_general(a, b, (((0,), (0,)), ((), ())), preferred_element_type=F32)


def tables(ids_ref):
    ids = [ids_ref[j : j + 1, :] for j in range(2)]
    lane = iota((N_E, TOK), 0)
    hits = [(i == lane).astype(F32) for i in ids]
    earlier = (iota((TOK, TOK), 0) < iota((TOK, TOK), 1)).astype(BF)
    rank = dot_nn((hits[0] + hits[1]).astype(BF), earlier)
    slot = iota((N_E * CAP, TOK), 0)
    out = []
    for j in range(2):
        place = jnp.sum(hits[j] * rank, axis=0, keepdims=True).astype(jnp.int32) + ids[j] * CAP
        out.append((slot == place).astype(F32))
    return out


def dispatch_kernel(ids_ref, gates_ref, tok_ref, cot_ref, out_ref):
    t0, t1 = tables(ids_ref)
    rows_in = dot_nn((t0 + t1).astype(BF), tok_ref[...]).astype(BF)
    rows_cot = jnp.zeros((N_E * CAP, LANE), F32)
    for j, table in enumerate((t0, t1)):
        gate = jnp.sum(table * gates_ref[j : j + 1, :], axis=1, keepdims=True)
        rows_cot = rows_cot + gate * dot_nn(table.astype(BF), cot_ref[...])
    rows_cot = rows_cot.astype(BF)
    for e in range(N_E):
        for q in range(N_Q):
            out_ref[e, q, 0:CAP] = rows_in[e * CAP : (e + 1) * CAP]
            out_ref[e, q, CAP : 2 * CAP] = rows_cot[e * CAP : (e + 1) * CAP]


def combine_kernel(ids_ref, gates_ref, back_ref, mixed_ref, grad_ref):
    t0, t1 = tables(ids_ref)
    total = back_ref[:, 0].astype(F32)
    for q in range(1, N_Q):
        total = total + back_ref[:, q].astype(F32)
    weighted = t0 * gates_ref[0:1, :] + t1 * gates_ref[1:2, :]
    for table, first, out_ref in ((weighted, 0, mixed_ref), (t0 + t1, CAP, grad_ref)):
        out_ref[...] = lax.dot_general(
            table,
            total[:, first : first + CAP].reshape(N_E * CAP, LANE),
            (((0,), (0,)), ((), ())),
            precision=lax.Precision.HIGHEST,
            preferred_element_type=F32,
        ).astype(BF)


def counts(marks_ref):
    upto = (iota((COLS, COLS), 0) <= iota((COLS, COLS), 1)).astype(BF)
    return dot_nn(marks_ref[...].astype(BF), upto)


def pick_row(values, row):
    return jnp.sum(jnp.where(iota(values.shape, 0) == row, values, 0.0), axis=0, keepdims=True)


def pack_kernel(where_ref, marks_ref, dense_ref, *outs):
    cum = counts(marks_ref)
    marks = marks_ref[...].astype(F32)
    col = iota((1, COLS), 1).astype(F32)
    dense = dense_ref[...]
    for k in range(N_X):
        expert = lax.rem(where_ref[0] + k, N_X) * 2 + where_ref[1]
        kept = jnp.where(pick_row(marks, expert) > 0.5, -1.0, col - pick_row(cum, expert))
        onehot = (iota((HALF, COLS), 0) == kept.astype(jnp.int32)).astype(BF)
        outs[k][...] = dot_nt(dense, onehot).astype(BF)


def order_of_units(where_ref, marks_ref):
    expert = where_ref[0] * 2 + where_ref[1]
    cum = pick_row(counts(marks_ref), expert)
    mark = pick_row(marks_ref[...].astype(F32), expert)
    col = iota((1, COLS), 1).astype(F32)
    source = jnp.where(mark > 0.5, HALF + cum - 1.0, col - cum).astype(jnp.int32)
    return (iota((COLS, COLS), 0) == source).astype(BF)


def slab_rows(rows_ref, z, first):
    return jnp.concatenate(
        [
            rows_ref[:, 0, z, q, first : first + CAP].reshape(ROWS, LANE)
            for q in range(N_Q)
        ],
        axis=1,
    )


def accumulate(step, accs, parts):
    @pl.when(step == 0)
    def _():
        for acc, part in zip(accs, parts):
            acc[...] = part

    @pl.when(step > 0)
    def _():
        for acc, part in zip(accs, parts):
            acc[...] += part


def far_piece(far, p, k):
    return far[p * N_X + k][...]


def expert_kernel(where_ref, rows_ref, fresh_ref, *refs):
    near, far, refs = refs[:N_X], refs[N_X : 4 * N_X], refs[4 * N_X :]
    hidden_ref, both_ref, out_ref, held, gate_acc, up_acc, down_acc = refs
    step = pl.program_id(0)
    z, other_z = where_ref[1], 1 - where_ref[1]

    for k in range(N_X):

        @pl.when(step == k)
        def _():
            for p in range(3):
                for side, (at, piece) in enumerate(((z, near[k][p]), (other_z, far_piece(far, p, k)))):
                    held[k, p, side * SLAB : (side + 1) * SLAB, :] = jnp.concatenate(
                        [piece, fresh_ref[p, 0, at]], axis=1
                    )

    @pl.when(step < N_X)
    def _():
        rows_in = jnp.concatenate([slab_rows(rows_ref, z, 0), slab_rows(rows_ref, other_z, 0)], axis=1)
        rows_cot = jnp.concatenate(
            [slab_rows(rows_ref, z, CAP), slab_rows(rows_ref, other_z, CAP)], axis=1
        )
        parts = [
            dot_nn(r, held[step, p]) for p, r in enumerate((rows_in, rows_in, rows_cot))
        ]
        accumulate(step, (gate_acc, up_acc, down_acc), parts)

    @pl.when(step == N_X - 1)
    def _():
        gate, up, grad = gate_acc[...], up_acc[...], down_acc[...]
        sig = jax.nn.sigmoid(gate)
        act = gate * sig
        hidden_ref[...] = (act * up).astype(BF)
        both_ref[:, 0:COLS] = (grad * up * sig * (1.0 + gate * (1.0 - sig))).astype(BF)
        both_ref[:, COLS:] = (grad * act).astype(BF)

    @pl.when(step >= N_X)
    def _():
        k = step - N_X
        pair = jnp.concatenate([held[k, 0], held[k, 1]], axis=1)
        outs = dot_nt(hidden_ref[...], held[k, 2]).astype(BF)
        grads = dot_nt(both_ref[...], pair).astype(BF)
        for first, values in ((0, outs), (CAP, grads)):
            for side, at in enumerate((z, other_z)):
                for q in range(N_Q):
                    lane = side * SLAB + q * LANE
                    out_ref[:, 0, at, q, first : first + CAP] = values[
                        :, lane : lane + LANE
                    ].reshape(N_DP, CAP, LANE)


def update_kernel(where_ref, rows_ref, fresh_ref, *refs):
    near, far, refs = refs[:N_X], refs[N_X : 4 * N_X], refs[4 * N_X :]
    hidden_ref, both_ref, marks_ref, new_ref, order, held = refs
    step = pl.program_id(0)

    @pl.when(step == 0)
    def _():
        order[...] = order_of_units(where_ref, marks_ref)

    for k in range(N_X):

        @pl.when(step == k)
        def _():
            for p in range(3):
                held[p, 0] = near[k][p]
                held[p, 1] = far_piece(far, p, k)

    for side, z in enumerate((where_ref[1], 1 - where_ref[1])):
        pair = dot_tn(slab_rows(rows_ref, z, 0), both_ref[...])
        down = dot_tn(slab_rows(rows_ref, z, CAP), hidden_ref[...])
        for p, g in enumerate((pair[:, 0:COLS], pair[:, COLS:], down)):
            w = jnp.concatenate([held[p, side], fresh_ref[p, 0, z]], axis=1).astype(F32)
            new = w * (1.0 - 0.0003) - 0.003 * (g / (jnp.abs(g) + 0.1))
            new_ref[p, 0, z] = dot_nn(new.astype(BF), order[...]).astype(BF)


def call(kernel, outs, prefetch=0, scratch=(), **kw):
    if "grid" in kw:
        kw = dict(
            grid_spec=pltpu.PrefetchScalarGridSpec(
                num_scalar_prefetch=prefetch, scratch_shapes=list(scratch), **kw
            )
        )
    return pl.pallas_call(
        kernel,
        out_shape=outs,
        compiler_params=pltpu.CompilerParams(vmem_limit_bytes=VMEM_CAP),
        cost_estimate=pl.CostEstimate(flops=COST, bytes_accessed=COST, transcendentals=0),
        **kw,
    )


COST = 1024


def sds(shape, dtype=BF):
    return jax.ShapeDtypeStruct(shape, dtype)


SMEM = pl.BlockSpec(memory_space=pltpu.SMEM)
VIEW = (N_X, 2, N_Q, 2 * CAP, LANE)


def block_x(k, w):
    return lax.rem(w[0] + N_X - k, N_X)


def front_step(i):
    return jnp.minimum(i, N_X - 1)


def back_step(i):
    return jnp.maximum(i - N_X, 0)


def rows_spec(step):
    return pl.BlockSpec(
        (N_DP, 1) + VIEW[1:], lambda i, w: (0, block_x(step(i), w), 0, 0, 0, 0)
    )


def whole_spec(shape):
    return pl.BlockSpec(shape, lambda i, w: (0,) * len(shape))


FRESH_SPEC = pl.BlockSpec(
    (3, 1, 2, SLAB, HALF), lambda i, w: (0, block_x(front_step(i), w), 0, 0, 0)
)


def after(values, *first):
    return lax.optimization_barrier((values, first))[0]


def on_device(tokens, cotangent, gates, expert_ids, dense_ffn, redrawn, redraw):
    expert = lax.axis_index("expert")
    x, z = expert // 2, expert % 2
    where = jnp.stack([x, z]).astype(jnp.int32)

    def along_x(piece, k):
        return lax.ppermute(
            piece, "expert", [(e, (e // 2 + k) % N_X * 2 + e % 2) for e in range(N_E)]
        )

    def other_side(slab):
        return lax.ppermute(slab, "expert", [(e, e ^ 1) for e in range(N_E)])

    def exchange(rows):
        return lax.all_to_all(rows, ("expert", "mp"), split_axis=0, concat_axis=0, tiled=True)

    def pack(slab):
        rows = slab.shape[0]
        return call(
            pack_kernel,
            [sds((rows, HALF))] * N_X,
            in_specs=[SMEM, pl.BlockSpec(), pl.BlockSpec()],
        )(where, redrawn, slab)

    def to_holders(packed):
        return [packed[0]] + [along_x(packed[k], k) for k in range(1, N_X)]

    ids, weights = expert_ids.T, gates.T
    slots = call(dispatch_kernel, sds((N_E, N_Q, 2 * CAP, LANE)))(ids, weights, tokens, cotangent)
    parts = [dense_ffn[p] for p in range(3)]
    near = pack(dense_ffn.reshape(3 * SLAB, COLS))
    slots, parts = lax.optimization_barrier((slots, parts))
    mine = exchange(slots.reshape(2 * PIECE, LANE))

    gate = other_side(parts[0])
    near = to_holders(near)
    mine, near, gate, parts = lax.optimization_barrier((mine, near, gate, parts))
    rows = lax.all_gather(mine, "dp", axis=0, tiled=True).reshape((N_DP,) + VIEW)
    up, down = other_side(parts[1]), other_side(parts[2])
    gate, up = lax.optimization_barrier((to_holders(pack(gate)), up))
    up = to_holders(pack(up))
    up[1], down = lax.optimization_barrier((up[1], down))
    pieces = [p.reshape(3, SLAB, HALF) for p in near] + gate + up + to_holders(pack(down))
    piece_specs = [whole_spec(p.shape) for p in pieces]
    fresh = redraw.reshape(3, N_X, 2, SLAB, HALF)

    acts = [sds((ROWS, COLS)), sds((ROWS, 2 * COLS))]
    act_specs = [whole_spec(a.shape) for a in acts]
    hidden, both, sums = call(
        expert_kernel,
        acts + [sds((N_DP,) + VIEW)],
        prefetch=1,
        scratch=[pltpu.VMEM((N_X, 3, 2 * SLAB, COLS), BF)] + [pltpu.VMEM((ROWS, COLS), F32)] * 3,
        grid=(2 * N_X,),
        in_specs=[rows_spec(front_step), FRESH_SPEC] + piece_specs,
        out_specs=act_specs + [rows_spec(back_step)],
    )(where, rows, fresh, *pieces)

    total = lax.psum_scatter(
        sums.reshape(N_DP * 2 * PIECE, LANE), "dp", scatter_dimension=0, tiled=True
    )
    new_weights = call(
        update_kernel,
        sds((3, N_X, 2, SLAB, COLS)),
        prefetch=1,
        scratch=[pltpu.VMEM((COLS, COLS), BF), pltpu.VMEM((3, 2, SLAB, HALF), BF)],
        grid=(N_X,),
        in_specs=[rows_spec(front_step), FRESH_SPEC]
        + piece_specs
        + act_specs
        + [whole_spec((N_E, COLS))],
        out_specs=pl.BlockSpec(
            (3, 1, 2, SLAB, COLS), lambda i, w: (0, block_x(i, w), 0, 0, 0)
        ),
    )(where, rows, fresh, *pieces, hidden, both, redrawn)
    back = exchange(total).reshape(N_E, N_Q, 2 * CAP, LANE)
    mixed, token_grad = call(combine_kernel, [sds((TOK, LANE))] * 2)(ids, weights, back)
    return (mixed, token_grad, new_weights.reshape(1, 3, N_E * SLAB, COLS))


def solution(mesh):
    return jax.shard_map(
        on_device,
        mesh=mesh,
        in_specs=(
            P("dp", ("expert", "mp")),
            P("dp", ("expert", "mp")),
            P("dp", None),
            P("dp", None),
            P(None, "expert", ("dp", "mp")),
            P(None, ("dp", "mp")),
            P("expert", None, None, ("dp", "mp")),
        ),
        out_specs=(
            P("dp", ("expert", "mp")),
            P("dp", ("expert", "mp")),
            P("expert", None, None, ("dp", "mp")),
        ),
        check_vma=False,
    )
```

```python
import jax
import jax.numpy as jnp
from jax import lax
from jax.experimental import pallas as pl
from jax.experimental.pallas import tpu as pltpu
from jax.sharding import PartitionSpec as P

BF = jnp.bfloat16
F32 = jnp.float32
CAP = 48
N_E = 8
N_DP = 8
N_X = 4
LANE = 128
COLS = 256
HALF = 128
SLAB = 512
TOK = 128
ROWS = N_DP * CAP
VMEM_CAP = 60 * 1024 * 1024
N_Y = 4
N_Q = 4
PIECE = N_E * N_Q * CAP


def iota(shape, dim):
    return lax.broadcasted_iota(jnp.int32, shape, dim)


def dot_nn(a, b):
    return lax.dot_general(a, b, (((1,), (0,)), ((), ())), preferred_element_type=F32)


def dot_nt(a, b):
    return lax.dot_general(a, b, (((1,), (1,)), ((), ())), preferred_element_type=F32)


def dot_tn(a, b):
    return lax.dot_general(a, b, (((0,), (0,)), ((), ())), preferred_element_type=F32)


def tables(ids_ref):
    ids = [ids_ref[j : j + 1, :] for j in range(2)]
    lane = iota((N_E, TOK), 0)
    hits = [(i == lane).astype(F32) for i in ids]
    earlier = (iota((TOK, TOK), 0) < iota((TOK, TOK), 1)).astype(BF)
    rank = dot_nn((hits[0] + hits[1]).astype(BF), earlier)
    slot = iota((N_E * CAP, TOK), 0)
    out = []
    for j in range(2):
        place = jnp.sum(hits[j] * rank, axis=0, keepdims=True).astype(jnp.int32) + ids[j] * CAP
        out.append((slot == place).astype(F32))
    return out


def dispatch_kernel(ids_ref, gates_ref, tok_ref, cot_ref, out_ref):
    t0, t1 = tables(ids_ref)
    rows_in = dot_nn((t0 + t1).astype(BF), tok_ref[...]).astype(BF)
    rows_cot = jnp.zeros((N_E * CAP, LANE), F32)
    for j, table in enumerate((t0, t1)):
        gate = jnp.sum(table * gates_ref[j : j + 1, :], axis=1, keepdims=True)
        rows_cot = rows_cot + gate * dot_nn(table.astype(BF), cot_ref[...])
    rows_cot = rows_cot.astype(BF)
    for e in range(N_E):
        for q in range(N_Q):
            out_ref[e, q, 0:CAP] = rows_in[e * CAP : (e + 1) * CAP]
            out_ref[e, q, CAP : 2 * CAP] = rows_cot[e * CAP : (e + 1) * CAP]


def combine_kernel(ids_ref, gates_ref, back_ref, mixed_ref, grad_ref):
    t0, t1 = tables(ids_ref)
    total = back_ref[:, 0].astype(F32)
    for q in range(1, N_Q):
        total = total + back_ref[:, q].astype(F32)
    weighted = t0 * gates_ref[0:1, :] + t1 * gates_ref[1:2, :]
    for table, first, out_ref in ((weighted, 0, mixed_ref), (t0 + t1, CAP, grad_ref)):
        out_ref[...] = lax.dot_general(
            table,
            total[:, first : first + CAP].reshape(N_E * CAP, LANE),
            (((0,), (0,)), ((), ())),
            precision=lax.Precision.HIGHEST,
            preferred_element_type=F32,
        ).astype(BF)


def counts(marks_ref):
    upto = (iota((COLS, COLS), 0) <= iota((COLS, COLS), 1)).astype(BF)
    return dot_nn(marks_ref[...].astype(BF), upto)


def pick_row(values, row):
    return jnp.sum(jnp.where(iota(values.shape, 0) == row, values, 0.0), axis=0, keepdims=True)


def pack_kernel(where_ref, marks_ref, dense_ref, *outs):
    cum = counts(marks_ref)
    marks = marks_ref[...].astype(F32)
    col = iota((1, COLS), 1).astype(F32)
    dense = dense_ref[...]
    for k in range(N_X):
        expert = lax.rem(where_ref[0] + k, N_X) * 2 + where_ref[1]
        kept = jnp.where(pick_row(marks, expert) > 0.5, -1.0, col - pick_row(cum, expert))
        onehot = (iota((HALF, COLS), 0) == kept.astype(jnp.int32)).astype(BF)
        outs[k][...] = dot_nt(dense, onehot).astype(BF)


def order_of_units(where_ref, marks_ref):
    expert = where_ref[0] * 2 + where_ref[1]
    cum = pick_row(counts(marks_ref), expert)
    mark = pick_row(marks_ref[...].astype(F32), expert)
    col = iota((1, COLS), 1).astype(F32)
    source = jnp.where(mark > 0.5, HALF + cum - 1.0, col - cum).astype(jnp.int32)
    return (iota((COLS, COLS), 0) == source).astype(BF)


def slab_rows(rows_ref, z, first):
    return jnp.concatenate(
        [
            rows_ref[:, 0, z, q, first : first + CAP].reshape(ROWS, LANE)
            for q in range(N_Q)
        ],
        axis=1,
    )


def accumulate(step, accs, parts):
    @pl.when(step == 0)
    def _():
        for acc, part in zip(accs, parts):
            acc[...] = part

    @pl.when(step > 0)
    def _():
        for acc, part in zip(accs, parts):
            acc[...] += part


def far_piece(far, p, k):
    return far[p * N_X + k][...]


def expert_kernel(where_ref, rows_ref, fresh_ref, *refs):
    near, far, refs = refs[:N_X], refs[N_X : 4 * N_X], refs[4 * N_X :]
    hidden_ref, both_ref, out_ref, held, gate_acc, up_acc, down_acc = refs
    step = pl.program_id(0)
    z, other_z = where_ref[1], 1 - where_ref[1]

    for k in range(N_X):

        @pl.when(step == k)
        def _():
            for p in range(3):
                for side, (at, piece) in enumerate(((z, near[k][p]), (other_z, far_piece(far, p, k)))):
                    held[k, p, side * SLAB : (side + 1) * SLAB, :] = jnp.concatenate(
                        [piece, fresh_ref[p, 0, at]], axis=1
                    )

    @pl.when(step < N_X)
    def _():
        rows_in = jnp.concatenate([slab_rows(rows_ref, z, 0), slab_rows(rows_ref, other_z, 0)], axis=1)
        rows_cot = jnp.concatenate(
            [slab_rows(rows_ref, z, CAP), slab_rows(rows_ref, other_z, CAP)], axis=1
        )
        parts = [
            dot_nn(r, held[step, p]) for p, r in enumerate((rows_in, rows_in, rows_cot))
        ]
        accumulate(step, (gate_acc, up_acc, down_acc), parts)

    @pl.when(step == N_X - 1)
    def _():
        gate, up, grad = gate_acc[...], up_acc[...], down_acc[...]
        sig = jax.nn.sigmoid(gate)
        act = gate * sig
        hidden_ref[...] = (act * up).astype(BF)
        both_ref[:, 0:COLS] = (grad * up * sig * (1.0 + gate * (1.0 - sig))).astype(BF)
        both_ref[:, COLS:] = (grad * act).astype(BF)

    @pl.when(step >= N_X)
    def _():
        k = step - N_X
        pair = jnp.concatenate([held[k, 0], held[k, 1]], axis=1)
        outs = dot_nt(hidden_ref[...], held[k, 2]).astype(BF)
        grads = dot_nt(both_ref[...], pair).astype(BF)
        for first, values in ((0, outs), (CAP, grads)):
            for side, at in enumerate((z, other_z)):
                for q in range(N_Q):
                    lane = side * SLAB + q * LANE
                    out_ref[:, 0, at, q, first : first + CAP] = values[
                        :, lane : lane + LANE
                    ].reshape(N_DP, CAP, LANE)


def update_kernel(where_ref, rows_ref, fresh_ref, *refs):
    near, far, refs = refs[:N_X], refs[N_X : 4 * N_X], refs[4 * N_X :]
    hidden_ref, both_ref, marks_ref, new_ref, order, held = refs
    step = pl.program_id(0)

    @pl.when(step == 0)
    def _():
        order[...] = order_of_units(where_ref, marks_ref)

    for k in range(N_X):

        @pl.when(step == k)
        def _():
            for p in range(3):
                held[p, 0] = near[k][p]
                held[p, 1] = far_piece(far, p, k)

    for side, z in enumerate((where_ref[1], 1 - where_ref[1])):
        pair = dot_tn(slab_rows(rows_ref, z, 0), both_ref[...])
        down = dot_tn(slab_rows(rows_ref, z, CAP), hidden_ref[...])
        for p, g in enumerate((pair[:, 0:COLS], pair[:, COLS:], down)):
            w = jnp.concatenate([held[p, side], fresh_ref[p, 0, z]], axis=1).astype(F32)
            new = w * (1.0 - 0.0003) - 0.003 * (g / (jnp.abs(g) + 0.1))
            new_ref[p, 0, z] = dot_nn(new.astype(BF), order[...]).astype(BF)


def call(kernel, outs, prefetch=0, scratch=(), **kw):
    if "grid" in kw:
        kw = dict(
            grid_spec=pltpu.PrefetchScalarGridSpec(
                num_scalar_prefetch=prefetch, scratch_shapes=list(scratch), **kw
            )
        )
    return pl.pallas_call(
        kernel,
        out_shape=outs,
        compiler_params=pltpu.CompilerParams(vmem_limit_bytes=VMEM_CAP),
        cost_estimate=pl.CostEstimate(flops=COST, bytes_accessed=COST, transcendentals=0),
        **kw,
    )


COST = 1024


def sds(shape, dtype=BF):
    return jax.ShapeDtypeStruct(shape, dtype)


SMEM = pl.BlockSpec(memory_space=pltpu.SMEM)
VIEW = (N_X, 2, N_Q, 2 * CAP, LANE)


def block_x(k, w):
    return lax.rem(w[0] + N_X - k, N_X)


def front_step(i):
    return jnp.minimum(i, N_X - 1)


def back_step(i):
    return jnp.maximum(i - N_X, 0)


def rows_spec(step):
    return pl.BlockSpec(
        (N_DP, 1) + VIEW[1:], lambda i, w: (0, block_x(step(i), w), 0, 0, 0, 0)
    )


def whole_spec(shape):
    return pl.BlockSpec(shape, lambda i, w: (0,) * len(shape))


FRESH_SPEC = pl.BlockSpec(
    (3, 1, 2, SLAB, HALF), lambda i, w: (0, block_x(front_step(i), w), 0, 0, 0)
)


def after(values, *first):
    return lax.optimization_barrier((values, first))[0]


def on_device(tokens, cotangent, gates, expert_ids, dense_ffn, redrawn, redraw):
    expert = lax.axis_index("expert")
    x, z = expert // 2, expert % 2
    where = jnp.stack([x, z]).astype(jnp.int32)

    def along_x(piece, k):
        return lax.ppermute(
            piece, "expert", [(e, (e // 2 + k) % N_X * 2 + e % 2) for e in range(N_E)]
        )

    def other_side(slab):
        return lax.ppermute(slab, "expert", [(e, e ^ 1) for e in range(N_E)])

    def exchange(rows):
        return lax.all_to_all(rows, ("expert", "mp"), split_axis=0, concat_axis=0, tiled=True)

    def pack(slab):
        rows = slab.shape[0]
        return call(
            pack_kernel,
            [sds((rows, HALF))] * N_X,
            in_specs=[SMEM, pl.BlockSpec(), pl.BlockSpec()],
        )(where, redrawn, slab)

    def to_holders(packed):
        return [packed[0]] + [along_x(packed[k], k) for k in range(1, N_X)]

    ids, weights = expert_ids.T, gates.T
    slots = call(dispatch_kernel, sds((N_E, N_Q, 2 * CAP, LANE)))(ids, weights, tokens, cotangent)
    parts = [dense_ffn[p] for p in range(3)]
    near = pack(dense_ffn.reshape(3 * SLAB, COLS))
    slots, parts = lax.optimization_barrier((slots, parts))
    mine = exchange(slots.reshape(2 * PIECE, LANE))

    gate = other_side(parts[0])
    near = to_holders(near)
    mine, near, gate, parts[2] = lax.optimization_barrier((mine, near, gate, parts[2]))
    rows = lax.all_gather(mine, "dp", axis=0, tiled=True).reshape((N_DP,) + VIEW)
    up, down = other_side(parts[1]), other_side(parts[2])
    gate, up = lax.optimization_barrier((to_holders(pack(gate)), up))
    up = to_holders(pack(up))
    up[1], down = lax.optimization_barrier((up[1], down))
    pieces = [p.reshape(3, SLAB, HALF) for p in near] + gate + up + to_holders(pack(down))
    piece_specs = [whole_spec(p.shape) for p in pieces]
    fresh = redraw.reshape(3, N_X, 2, SLAB, HALF)

    acts = [sds((ROWS, COLS)), sds((ROWS, 2 * COLS))]
    act_specs = [whole_spec(a.shape) for a in acts]
    hidden, both, sums = call(
        expert_kernel,
        acts + [sds((N_DP,) + VIEW)],
        prefetch=1,
        scratch=[pltpu.VMEM((N_X, 3, 2 * SLAB, COLS), BF)] + [pltpu.VMEM((ROWS, COLS), F32)] * 3,
        grid=(2 * N_X,),
        in_specs=[rows_spec(front_step), FRESH_SPEC] + piece_specs,
        out_specs=act_specs + [rows_spec(back_step)],
    )(where, rows, fresh, *pieces)

    total = lax.psum_scatter(
        sums.reshape(N_DP * 2 * PIECE, LANE), "dp", scatter_dimension=0, tiled=True
    )
    new_weights = call(
        update_kernel,
        sds((3, N_X, 2, SLAB, COLS)),
        prefetch=1,
        scratch=[pltpu.VMEM((COLS, COLS), BF), pltpu.VMEM((3, 2, SLAB, HALF), BF)],
        grid=(N_X,),
        in_specs=[rows_spec(front_step), FRESH_SPEC]
        + piece_specs
        + act_specs
        + [whole_spec((N_E, COLS))],
        out_specs=pl.BlockSpec(
            (3, 1, 2, SLAB, COLS), lambda i, w: (0, block_x(i, w), 0, 0, 0)
        ),
    )(where, rows, fresh, *pieces, hidden, both, redrawn)
    back = exchange(total).reshape(N_E, N_Q, 2 * CAP, LANE)
    mixed, token_grad = call(combine_kernel, [sds((TOK, LANE))] * 2)(ids, weights, back)
    return (mixed, token_grad, new_weights.reshape(1, 3, N_E * SLAB, COLS))


def solution(mesh):
    return jax.shard_map(
        on_device,
        mesh=mesh,
        in_specs=(
            P("dp", ("expert", "mp")),
            P("dp", ("expert", "mp")),
            P("dp", None),
            P("dp", None),
            P(None, "expert", ("dp", "mp")),
            P(None, ("dp", "mp")),
            P("expert", None, None, ("dp", "mp")),
        ),
        out_specs=(
            P("dp", ("expert", "mp")),
            P("dp", ("expert", "mp")),
            P("expert", None, None, ("dp", "mp")),
        ),
        check_vma=False,
    )
```
